32 devices in a mesh: row: 4 (over y, x), col: 8 (over z, core).
Axes of the slice: x: 2, y: 2, z: 4, core: 2. Of those that a mesh axis runs over, the one named last changes fastest.
Arguments:
- amplitudes: float32 [128, 128, 6144], P('col', 'row'), may hold values from -6 to 6
- integrals: float32 [6144, 6144], P('col', 'row'), may hold values from -0.078125 to 0.078125
- amp_pattern: int32 [128, 48], P('col'), may hold values 0 or 1
- int_pattern: int32 [48, 48], P(None, 'row'), may hold values from 0 to 1
Outputs:
- ladder: float32 [128, 128, 6144], P('col', 'row')
The draws below stay inside these ranges and needn't reach their ends.
All inputs are finite; a program needn't handle non-finite values. No bound on the sum of `amp_pattern` on one device may be relied on, other than what follows from the above.
Results may differ from the reference program's by a relative error of at most 0.00007.
Values sent between devices are 32-bit elements; how exact they have to be, the bound alone decides.
No kernel may reach another device: no remote copies, remote signals or barrier semaphores. Data moves between devices by JAX's collectives and lax.ppermute only.
A program may use at most 256 MiB of HBM per device.

```python
import jax
import jax.numpy as jnp
from jax import lax

OCC = 128
TILE = 128
KTILES = 48
NTILES = 48
KDIM = 6144
NDIM = 6144


def draw_int_pattern(key, part):
    tile_index = lax.broadcasted_iota(jnp.int32, (KTILES, NTILES), 1)
    drawn = jax.random.randint(key, (KTILES, NTILES), 0, NTILES)
    return (drawn <= tile_index).astype(jnp.int32)


def set_ends(values, key, least, largest):
    longest = values.shape.index(max(values.shape))
    spots = []
    for shift in (0, 1):
        where = [jax.random.randint(jax.random.fold_in(key, axis), (), 0, length) for axis, length in enumerate(values.shape)]
        where[longest] = (where[longest] + shift) % values.shape[longest]
        spots.append(tuple(where))
    return values.at[spots[0]].set(least).at[spots[1]].set(largest)


def levels(stream_key, extent, split, smallest, top_value):
    factor_of = 1.0
    for position, shards_of in split:
        draws = jax.random.uniform(jax.random.fold_in(jax.random.fold_in(stream_key, 6), position), (shards_of,), jnp.float32, smallest / len(split), top_value / len(split))
        factor_of = factor_of * jnp.repeat(jnp.exp(draws), extent[position] // shards_of).reshape((-1,) + (1,) * (len(extent) - 1 - position))
    return factor_of


def normal_values(key, shape, scale, limit, shards=(), dtype=jnp.bfloat16):
    gain = levels(key, shape, shards, -0.22, 0.18) if shards else 1.0
    values = jax.random.normal(key, shape, jnp.float32) * scale * gain
    return jnp.minimum(jnp.maximum(values, -limit), limit).astype(dtype)


def setup_inputs(seed: int = 0) -> dict:
    seeds = jax.random.split(jax.random.key(seed), 5)
    amplitudes = normal_values(seeds[0], (OCC, OCC, KDIM), 1.0, 6.0, ((0, 8), (1, 4)), jnp.float32)
    integrals = normal_values(seeds[1], (KDIM, NDIM), KDIM ** -0.5, 0.078125, ((0, 8), (1, 4)), jnp.float32)
    amp_pattern = set_ends((jax.random.randint(seeds[2], (OCC, KTILES), 0, 2) < 1).astype(jnp.int32), jax.random.fold_in(seeds[2], 1), 0, 1)
    int_pattern = draw_int_pattern(jax.random.fold_in(seeds[4], 71), 0)
    return {"amplitudes": amplitudes, "integrals": integrals, "amp_pattern": amp_pattern, "int_pattern": int_pattern}


def reference(amplitudes, integrals, amp_pattern, int_pattern):
    amp_mask = amp_pattern.astype(jnp.float32)
    int_mask = int_pattern.astype(jnp.float32)
    sparse_amp = (amplitudes.reshape(OCC, OCC, KTILES, TILE) * amp_mask[:, None, :, None]).reshape(OCC, OCC, KDIM)
    sparse_int = (integrals.reshape(KTILES, TILE, NTILES, TILE) * int_mask[:, None, :, None]).reshape(KDIM, NDIM)

    def one_index(block):
        return jnp.dot(block, sparse_int, precision=lax.Precision.HIGHEST, preferred_element_type=jnp.float32)

    return lax.map(one_index, sparse_amp)
```

```python
import functools

import jax
import jax.numpy as jnp
from jax import lax
from jax.experimental import pallas as pl
from jax.experimental.pallas import tpu as pltpu
from jax.sharding import PartitionSpec as P

TILE = 128
CORES = 2
UNROLL = 3
VMEM_LIMIT = 48 * 1024 * 1024


def split_kernel(mine_pattern, other_pattern, mine_ref, other_ref, out_ref, *, second):
    k = pl.program_id(0)
    rows = mine_ref.shape[0]
    for half, (pattern, amp_ref) in enumerate(((mine_pattern, mine_ref), (other_pattern, other_ref))):
        for first in range(rows // second):
            value = amp_ref[pl.ds(first * second, second), :] * pattern[first, k].astype(jnp.float32)
            high = value.astype(jnp.bfloat16)
            low = (value - high.astype(jnp.float32)).astype(jnp.bfloat16)
            here = pl.ds(half * rows + first * second, second)
            out_ref[0, here, :TILE] = high
            out_ref[0, here, TILE:] = low


def split_amplitudes(mine, other, mine_pattern, other_pattern, second):
    rows, depth = mine.shape
    tiles = depth // TILE
    return pl.pallas_call(
        functools.partial(split_kernel, second=second),
        grid_spec=pltpu.PrefetchScalarGridSpec(
            num_scalar_prefetch=2,
            grid=(tiles,),
            in_specs=[pl.BlockSpec((rows, TILE), lambda k, *_: (0, k))] * 2,
            out_specs=pl.BlockSpec((1, CORES * rows, 2 * TILE), lambda k, *_: (k, 0, 0)),
        ),
        out_shape=jax.ShapeDtypeStruct((tiles, CORES * rows, 2 * TILE), jnp.bfloat16),
        compiler_params=pltpu.CompilerParams(vmem_limit_bytes=VMEM_LIMIT),
        cost_estimate=pl.CostEstimate(flops=8 * rows * depth, bytes_accessed=16 * rows * depth, transcendentals=0),
    )(mine_pattern, other_pattern, mine, other)


def pack_kernel(source_ref, row_ref, lane_ref, *refs, plan, sources):
    ins, outs = refs[:sources], refs[sources:]
    for out, (base, size) in zip(outs, plan):

        def copy(slot, _, out=out, base=base):
            row = pl.multiple_of(row_ref[base + slot], TILE)
            lane = pl.multiple_of(lane_ref[base + slot], TILE)
            for source in range(sources):

                @pl.when(source_ref[base + slot] == source)
                def _(source=source):
                    out[slot] = ins[source][pl.ds(row, TILE), pl.ds(lane, TILE)]

            return 0

        lax.fori_loop(0, size, copy, 0)


def pack(scalars, sources, plan):
    whole = lambda x: pl.BlockSpec(x.shape, lambda g, *s: (0,) * len(x.shape))
    outs = [jax.ShapeDtypeStruct((size, TILE, TILE), jnp.float32) for _, size in plan]
    return pl.pallas_call(
        functools.partial(pack_kernel, plan=plan, sources=len(sources)),
        grid_spec=pltpu.PrefetchScalarGridSpec(
            num_scalar_prefetch=len(scalars),
            grid=(1,),
            in_specs=[whole(x) for x in sources],
            out_specs=[whole(x) for x in outs],
        ),
        out_shape=outs,
        compiler_params=pltpu.CompilerParams(vmem_limit_bytes=VMEM_LIMIT),
        cost_estimate=pl.CostEstimate(
            flops=0, bytes_accessed=4 * (sum(x.size for x in sources) + sum(x.size for x in outs)), transcendentals=0
        ),
    )(*scalars, *sources)


def pool_kernel(sizes_ref, offsets_ref, *refs, segments):
    count = sum(len(parts) for parts in segments)
    ins, out, sem = refs[:count], refs[count], refs[count + 1]
    for waiting in (False, True):
        at = 0
        for e, parts in enumerate(segments):
            for a, b in parts:
                ref = ins[at]
                at += 1

                def step(slot, _, ref=ref, a=a, e=e):
                    place = offsets_ref[e] + slot
                    copy = pltpu.make_async_copy(ref.at[slot - a], out.at[place], sem.at[place])
                    if waiting:
                        copy.wait()
                    else:
                        copy.start()
                    return 0

                lax.fori_loop(a, jnp.maximum(a, jnp.minimum(b, sizes_ref[e])), step, 0)


def pool(sizes, offsets, pieces, capacity):
    arrays = [x for parts in pieces for x, _, _ in parts]
    segments = [[(a, b) for _, a, b in parts] for parts in pieces]
    return pl.pallas_call(
        functools.partial(pool_kernel, segments=segments),
        grid_spec=pltpu.PrefetchScalarGridSpec(
            num_scalar_prefetch=2,
            grid=(1,),
            in_specs=[pl.BlockSpec(memory_space=pl.ANY)] * len(arrays),
            out_specs=pl.BlockSpec(memory_space=pl.ANY),
            scratch_shapes=[pltpu.SemaphoreType.DMA((capacity,))],
        ),
        out_shape=jax.ShapeDtypeStruct((capacity, TILE, TILE), jnp.float32),
        compiler_params=pltpu.CompilerParams(vmem_limit_bytes=VMEM_LIMIT),
        cost_estimate=pl.CostEstimate(flops=0, bytes_accessed=8 * capacity * TILE * TILE, transcendentals=0),
    )(sizes, offsets, *arrays)


def gate_kernel(*refs):
    del refs


def gate(released, awaited):
    anywhere = pl.BlockSpec(memory_space=pl.ANY)
    return pl.pallas_call(
        gate_kernel,
        in_specs=[anywhere] * (len(released) + len(awaited)),
        out_specs=[anywhere] * len(released),
        out_shape=[jax.ShapeDtypeStruct(x.shape, x.dtype) for x in released],
        input_output_aliases={i: i for i in range(len(released))},
    )(*released, *awaited)


def multiply_kernel(
    plane_ref, low_ref, high_ref, shift_ref, base_ref, mine_at, other_at, fresh_ref, kk_ref, amp_ref, mine_in, other_in, *refs,
    segments, passed, steps, per_chip,
):
    count = len(segments)
    tiles = refs[:count]
    refs = refs[count + passed :]
    mine_ref, other_ref = refs[:2]
    buffer, sem = refs[2 + passed :]
    step = pl.program_id(0)
    rows = mine_ref.shape[0]

    def issue(g, half):
        low, high = low_ref[g], high_ref[g]
        for ref, (a, b, pooled, only) in zip(tiles, segments):
            shift = shift_ref[g] if pooled else -a

            def start(slot, _, ref=ref, shift=shift):
                pltpu.make_async_copy(
                    ref.at[slot + shift], buffer.at[half, slot - low], sem.at[half, slot - low]
                ).start()
                return 0

            first = jnp.maximum(low, a)
            last = jnp.maximum(first, jnp.minimum(high, b))
            if only is not None:
                last = jnp.where(g // per_chip == only, last, first)
            lax.fori_loop(first, last, start, 0)

    half = lax.rem(step, 2)

    @pl.when(step == 0)
    def _():
        issue(0, 0)

    @pl.when(step + 1 < steps)
    def _():
        issue(step + 1, 1 - half)

    @pl.when(fresh_ref[step] > 0)
    def _():
        mine_ref[...] = mine_in[...]
        other_ref[...] = other_in[...]

    low = low_ref[step]
    length = high_ref[step] - low
    base = base_ref[step] + low

    def wait(at, _):
        pltpu.make_async_copy(tiles[0].at[0], buffer.at[half, at], sem.at[half, at]).wait()
        return 0

    lax.fori_loop(0, length, wait, 0)

    def add(turn, _):
        weights, ks = [], []
        for u in range(UNROLL):
            at = turn * UNROLL + u
            inside = at < length
            at = jnp.minimum(at, length - 1)
            value = buffer[half, at]
            if u:
                value = jnp.where(inside, value, 0.0)
            high = value.astype(jnp.bfloat16)
            rest = (value - high.astype(jnp.float32)).astype(jnp.bfloat16)
            weights.append(jnp.concatenate([high, rest], axis=1))
            weights.append(jnp.concatenate([high, jnp.zeros_like(high)], axis=1))
            ks.append(kk_ref[base + at])
        left = jnp.concatenate([amp_ref[k] for k in ks], axis=1)
        product = jnp.dot(left, jnp.concatenate(weights, axis=0), preferred_element_type=jnp.float32)
        total = product[:, :TILE] + product[:, TILE:]
        mine_ref[...] += total[:rows]
        other_ref[...] += total[rows:]
        return 0

    lax.fori_loop(0, (length + UNROLL - 1) // UNROLL, add, 0)


def multiply(scalars, steps, per_chip, amps, mine, other, pieces, kd, released=()):
    rows = mine.shape[0]
    segments = [piece[1:] for piece in pieces]
    expected = 10 * steps
    n = len(scalars)
    mine_spec = pl.BlockSpec((rows, TILE), lambda g, *s: (0, s[5][g]))
    other_spec = pl.BlockSpec((rows, TILE), lambda g, *s: (0, s[6][g]))
    anywhere = pl.BlockSpec(memory_space=pl.ANY)
    first = n + 3 + len(pieces)
    aliases = {n + 1: 0, n + 2: 1}
    aliases.update({first + i: 2 + i for i in range(len(released))})
    return pl.pallas_call(
        functools.partial(multiply_kernel, segments=segments, passed=len(released), steps=steps, per_chip=per_chip),
        grid_spec=pltpu.PrefetchScalarGridSpec(
            num_scalar_prefetch=n,
            grid=(steps,),
            in_specs=[
                pl.BlockSpec((CORES * kd, CORES * rows, 2 * TILE), lambda g, *s: (s[0][0], 0, 0)),
                mine_spec,
                other_spec,
            ]
            + [anywhere] * (len(pieces) + len(released)),
            out_specs=[mine_spec, other_spec] + [anywhere] * len(released),
            scratch_shapes=[
                pltpu.VMEM((2, CORES * kd, TILE, TILE), jnp.float32),
                pltpu.SemaphoreType.DMA((2, CORES * kd)),
            ],
        ),
        out_shape=[jax.ShapeDtypeStruct(x.shape, x.dtype) for x in (mine, other, *released)],
        input_output_aliases=aliases,
        compiler_params=pltpu.CompilerParams(vmem_limit_bytes=VMEM_LIMIT),
        cost_estimate=pl.CostEstimate(
            flops=expected * 32 * rows * TILE * TILE,
            bytes_accessed=expected * 4 * TILE * TILE,
            transcendentals=0,
        ),
    )(*scalars, amps, mine, other, *[piece[0] for piece in pieces], *released)


def place_kernel(at_ref, mine_in, piece_ref, out_ref):
    out_ref[...] = mine_in[...] + piece_ref[...]


def place(at, mine, piece):
    rows = mine.shape[0]
    spec = pl.BlockSpec((rows, TILE), lambda g, a: (0, a[g]))
    return pl.pallas_call(
        place_kernel,
        grid_spec=pltpu.PrefetchScalarGridSpec(
            num_scalar_prefetch=1,
            grid=(at.shape[0],),
            in_specs=[spec, pl.BlockSpec((rows, TILE), lambda g, a: (0, g))],
            out_specs=spec,
        ),
        out_shape=jax.ShapeDtypeStruct(mine.shape, mine.dtype),
        input_output_aliases={1: 0},
        compiler_params=pltpu.CompilerParams(vmem_limit_bytes=VMEM_LIMIT),
        cost_estimate=pl.CostEstimate(flops=piece.size, bytes_accessed=12 * piece.size, transcendentals=0),
    )(at, mine, piece)


def body(amplitudes, integrals, amp_pattern, int_pattern, *, chips, devices):
    R, Z = chips, devices // CORES
    first, second, depth = amplitudes.shape
    rows = first * second
    kd = integrals.shape[0] // TILE
    ntl = integrals.shape[1] // TILE
    groups = R if ntl % R == 0 else 1
    width = ntl // groups
    per_chip = -(-ntl // CORES)
    tiles = per_chip * CORES * kd

    r = lax.axis_index("row")
    col = lax.axis_index("col")
    core = lax.rem(col, CORES)
    ring = [0] + list(range(1, Z, 2)) + [z for z in range(Z - 1, 0, -1) if z % 2 == 0]
    spot = [ring.index(z) for z in range(Z)]

    def by_row(x, distance):
        return lax.ppermute(x, "row", [(a, a ^ distance) for a in range(R)])

    def by_core(x):
        return lax.ppermute(x, "col", [(a, a ^ 1) for a in range(Z * CORES)])

    def by_plane(x):
        return lax.ppermute(
            x,
            "col",
            [(ring[a] * CORES + c, ring[(a + 1) % Z] * CORES + c) for a in range(Z) for c in range(CORES)],
        )

    shares = [integrals[:, : width * TILE] if groups > 1 else integrals]
    for d in range(1, groups):
        shares.append(by_row(integrals[:, d * width * TILE : (d + 1) * width * TILE], d))

    amps_mine = amplitudes.reshape(rows, depth)
    amps = split_amplitudes(amps_mine, by_core(amps_mine), amp_pattern, by_core(amp_pattern), second)
    mine = jnp.zeros((rows, (R * ntl + per_chip * CORES - ntl) * TILE), jnp.float32)
    if groups > 1:
        *shares[1:], mine = gate([*shares[1:], mine], [amps])
    twins = [by_core(x) for x in shares]

    patterns = [int_pattern] + [by_row(int_pattern, d) for d in range(1, R)]
    by_distance = jnp.stack(patterns).reshape(R, Z, CORES * kd, groups, width)
    near = []
    for e in range(R):
        picked = jnp.stack([by_distance[e ^ d, :, :, d] for d in range(groups)], axis=2)
        near.append(picked.reshape(Z, CORES * kd, ntl))
    present = (jnp.stack(near, axis=1) != 0).astype(jnp.int32)
    present = jnp.pad(present, ((0, 0), (0, 0), (0, 0), (0, per_chip * CORES - ntl)))
    present = present.reshape(Z, R, CORES * kd, per_chip, CORES).transpose(0, 1, 4, 3, 2)
    both = present.reshape(Z, R, CORES, tiles)
    cores_counts = jnp.sum(both, axis=-1)
    own = jnp.where(core == 0, both[:, :, 0], both[:, :, 1])
    here = jnp.asarray(spot)[col // CORES]
    planes = jnp.asarray(ring)[lax.rem(here - jnp.arange(Z) + Z, Z)]
    if R == 4:
        own = jnp.stack(
            [
                own[:, 0],
                jnp.where(core == 0, own[:, 1], own[:, 2]),
                jnp.where(core == 0, own[:, 2], own[:, 1]),
                own[:, 3],
            ],
            axis=1,
        )
    own = own[planes]
    counts = jnp.sum(own, axis=-1)
    ids = jnp.arange(tiles)
    slot_of = jnp.sum(own[..., None, :] * (ids[None, :] < ids[:, None]), axis=-1)
    slots = (
        jnp.sum(
            (ids + 1)[None, None, None, :]
            * ((slot_of[:, :, None, :] == ids[:, None]) & (own[:, :, None, :] > 0)),
            axis=-1,
        )
        - 1
    )
    ends = jnp.sum(own[:, :, None, :] * (ids[None, :] < (jnp.arange(per_chip + 1) * CORES * kd)[:, None]), axis=-1)

    straight = max(2, round(tiles * 35 / 72)) if R == 4 else max(4, 2 * round(tiles * 25 / 72))
    extra = max(2, round(tiles * 16 / 72)) if R == 4 else 0
    pooled = max(R, round(tiles * 32 / 72)) if R == 4 else 0
    longest = tiles + straight + extra
    slots = jnp.pad(slots, ((0, 0), (0, 0), (0, longest - tiles)), constant_values=-1)
    most = jnp.max(cores_counts)

    def chips_of(which):
        return r ^ (jnp.stack([0 * which, 1 + which, 2 - which, 0 * which + 3]) if R == 4 else jnp.arange(R))

    chip_of = chips_of(core)
    blocks = R * ntl
    spare = per_chip * CORES - ntl

    def columns_of(which):
        column = jnp.arange(per_chip)[None, :] * CORES + which
        group = column // width
        chip = chips_of(which)[:, None]
        at = (((chip ^ group) if groups > 1 else chip) * groups + group) * width + column % width
        return jnp.where(column < ntl, at, blocks).astype(jnp.int32)

    mine_at = columns_of(core)
    received_at = columns_of(1 - core)

    def across(x, near):
        return lax.ppermute(
            x,
            ("row", "col"),
            [
                (a * devices + d, (a ^ (near if d % CORES == 0 else 3 - near)) * devices + d)
                for a in range(R)
                for d in range(devices)
            ],
        )

    def one_round(state):
        base, mine = state
        after = base + straight
        left = jnp.clip(cores_counts - after, 0, extra)
        fits = jnp.max(jnp.sum(left, axis=1)) <= pooled
        taken = jnp.where(fits, extra, pooled // R) if extra else jnp.int32(0)
        sizes = jnp.clip(counts - after, 0, taken)
        before = chip_of[None, :] < chip_of[:, None]
        offsets = jnp.sum(sizes[:, None, :] * before[None], axis=-1).astype(jnp.int32)
        now = lax.dynamic_slice_in_dim(slots, base, straight + extra, axis=2)
        kk = jnp.maximum(now, 0) % (CORES * kd)
        bounds = jnp.clip(ends - base, 0, straight + taken).astype(jnp.int32)

        column = now[0, 0] // (CORES * kd) * CORES + core
        holder = kk[0, 0] // kd
        source = jnp.where(now[0, 0] < 0, -1, (holder != core) * groups + column // width)
        where = [source, kk[0, 0] % kd * TILE, column % width * TILE]
        plan = ((0, straight), (straight, extra), (0, straight)) if extra else ((0, straight),)
        packed = pack([x.astype(jnp.int32) for x in where], shares + twins, plan)

        other = jnp.zeros((rows, R * per_chip * TILE), jnp.float32)

        def add(mine, other, step, neighbours, low_slot, high_slot, pieces, released=(), sparse=False):
            low, high, shift, base_at = [], [], [], []
            for e in neighbours:
                limits = jnp.clip(bounds[step, e], low_slot, high_slot)
                low.append(limits[:-1])
                high.append(limits[1:])
                shift.append(jnp.broadcast_to(offsets[step, e] - straight, (per_chip,)))
                base_at.append(jnp.full((per_chip,), (e - neighbours[0]) * (straight + extra)))
            first_e, last_e = neighbours[0], neighbours[-1] + 1
            lists = [jnp.concatenate(x) for x in (low, high, shift, base_at)]
            lists.append(mine_at[first_e:last_e].reshape(-1))
            lists.append(jnp.arange(first_e * per_chip, last_e * per_chip))
            steps = len(neighbours) * per_chip
            if sparse:
                full = lists[1] > lists[0]
                ids = jnp.arange(steps)
                spots = jnp.sum(full[None, :] & (ids[None, :] < ids[:, None]), axis=1)
                taken_spot = jnp.minimum(ids, jnp.maximum(jnp.sum(full) - 1, 0))
                chosen = (spots[None, :] == taken_spot[:, None]) & full[None, :]
                lists = [jnp.sum(jnp.where(chosen, x[None, :], 0), axis=1) for x in lists]
                fresh = (ids == 0) | (ids < jnp.sum(full))
                lists[1] = jnp.where(fresh, lists[1], lists[0])
            else:
                fresh = jnp.ones((steps,), jnp.int32)
            lists.append(fresh)
            scalars = [planes[step].reshape(1), *lists, kk[step, first_e:last_e].reshape(-1)]
            scalars = [x.astype(jnp.int32) for x in scalars]
            return multiply(scalars, steps, per_chip, amps, mine, other, pieces, kd, released)

        if R == 4:
            end = straight + extra
            sent, late = packed[0], packed[1]
            along = [sent, by_plane(sent)]
            first_late, second_late = across(late, 1), across(late, 2)
            at_home = [(sent, 0, straight, False, None), (late, straight, end, False, None)]
            mine, other = add(mine, other, 0, [0], 0, end, at_home)
            third_late = across(first_late, 2)
            spare_sent, mine = gate([packed[2], mine], [third_late])
            first_near, second_near = across(spare_sent, 1), across(spare_sent, 2)
            pools = [
                pool(
                    sizes[0].astype(jnp.int32),
                    offsets[0],
                    [[(x, 0, extra)] for x in (late, first_late, second_late, third_late)],
                    pooled,
                )
            ]
            pools.append(by_plane(pools[0]))
            block = per_chip * TILE
            received = []
            for step in range(Z):
                mixed = (pools[step], straight, end, True, None)
                if step:
                    mine, other = add(mine, other, step, [0], 0, end, [(along[step], 0, straight, False, None), mixed])
                if step == Z - 1:
                    received.append(by_core(other[:, :block]))
                third_near = across(first_near, 2)
                near = [(first_near, 0, straight, False, 0), (second_near, 0, straight, False, 1), mixed]
                if step + 1 < Z:
                    along[step + 1], mine = gate([along[step + 1], mine], [first_near, second_near])
                    first_near, second_near = across(along[step + 1], 1), across(along[step + 1], 2)
                    if step + 2 < Z:
                        along.append(by_plane(along[step + 1]))
                        pools.append(by_plane(pools[step + 1]))
                mine, other = add(mine, other, step, [1, 2], 0, end, near)
                if step == Z - 1:
                    received.append(by_core(other[:, block : 3 * block]))
                    mine = place(received_at[0], mine, received[0])
                mine, other = add(mine, other, step, [3], 0, end, [(third_near, 0, straight, False, None), mixed])
            received.append(by_core(other[:, 3 * block :]))
            mine = place(received_at[1:3].reshape(-1), mine, received[1])
            mine = place(received_at[3], mine, received[2])
        else:
            now_at = packed[0]
            for step in range(Z):
                for e in range(R):
                    piece = by_row(now_at, e) if e else now_at
                    mine, other = add(mine, other, step, [e], 0, straight, [(piece, 0, straight, False, None)])
                if step + 1 < Z:
                    now_at = by_plane(now_at)
            mine = place(received_at.reshape(-1), mine, by_core(other))
        return base + straight + taken, mine

    state = one_round((jnp.int32(0), mine))
    _, mine = lax.while_loop(lambda state: state[0] < most, one_round, state)
    return mine[:, : blocks * TILE].reshape(first, second, blocks * TILE)


def solution(mesh):
    placed = (P("col", "row", None), P("col", "row"), P("col", None), P(None, "row"))
    return jax.shard_map(
        functools.partial(body, chips=mesh.shape["row"], devices=mesh.shape["col"]),
        mesh=mesh,
        in_specs=placed,
        out_specs=P("col", "row", None),
        check_vma=False,
    )
```

```python
import functools

import jax
import jax.numpy as jnp
from jax import lax
from jax.experimental import pallas as pl
from jax.experimental.pallas import tpu as pltpu
from jax.sharding import PartitionSpec as P

TILE = 128
CORES = 2
UNROLL = 3
VMEM_LIMIT = 48 * 1024 * 1024


def split_kernel(mine_pattern, other_pattern, mine_ref, other_ref, out_ref, *, second):
    k = pl.program_id(0)
    rows = mine_ref.shape[0]
    for half, (pattern, amp_ref) in enumerate(((mine_pattern, mine_ref), (other_pattern, other_ref))):
        for first in range(rows // second):
            value = amp_ref[pl.ds(first * second, second), :] * pattern[first, k].astype(jnp.float32)
            high = value.astype(jnp.bfloat16)
            low = (value - high.astype(jnp.float32)).astype(jnp.bfloat16)
            here = pl.ds(half * rows + first * second, second)
            out_ref[0, here, :TILE] = high
            out_ref[0, here, TILE:] = low


def split_amplitudes(mine, other, mine_pattern, other_pattern, second):
    rows, depth = mine.shape
    tiles = depth // TILE
    return pl.pallas_call(
        functools.partial(split_kernel, second=second),
        grid_spec=pltpu.PrefetchScalarGridSpec(
            num_scalar_prefetch=2,
            grid=(tiles,),
            in_specs=[pl.BlockSpec((rows, TILE), lambda k, *_: (0, k))] * 2,
            out_specs=pl.BlockSpec((1, CORES * rows, 2 * TILE), lambda k, *_: (k, 0, 0)),
        ),
        out_shape=jax.ShapeDtypeStruct((tiles, CORES * rows, 2 * TILE), jnp.bfloat16),
        compiler_params=pltpu.CompilerParams(vmem_limit_bytes=VMEM_LIMIT),
        cost_estimate=pl.CostEstimate(flops=8 * rows * depth, bytes_accessed=16 * rows * depth, transcendentals=0),
    )(mine_pattern, other_pattern, mine, other)


def pack_kernel(source_ref, row_ref, lane_ref, *refs, plan, sources):
    ins, outs = refs[:sources], refs[sources:]
    for out, (base, size) in zip(outs, plan):

        def copy(slot, _, out=out, base=base):
            row = pl.multiple_of(row_ref[base + slot], TILE)
            lane = pl.multiple_of(lane_ref[base + slot], TILE)
            for source in range(sources):

                @pl.when(source_ref[base + slot] == source)
                def _(source=source):
                    out[slot] = ins[source][pl.ds(row, TILE), pl.ds(lane, TILE)]

            return 0

        lax.fori_loop(0, size, copy, 0)


def pack(scalars, sources, plan):
    whole = lambda x: pl.BlockSpec(x.shape, lambda g, *s: (0,) * len(x.shape))
    outs = [jax.ShapeDtypeStruct((size, TILE, TILE), jnp.float32) for _, size in plan]
    return pl.pallas_call(
        functools.partial(pack_kernel, plan=plan, sources=len(sources)),
        grid_spec=pltpu.PrefetchScalarGridSpec(
            num_scalar_prefetch=len(scalars),
            grid=(1,),
            in_specs=[whole(x) for x in sources],
            out_specs=[whole(x) for x in outs],
        ),
        out_shape=outs,
        compiler_params=pltpu.CompilerParams(vmem_limit_bytes=VMEM_LIMIT),
        cost_estimate=pl.CostEstimate(
            flops=0, bytes_accessed=4 * (sum(x.size for x in sources) + sum(x.size for x in outs)), transcendentals=0
        ),
    )(*scalars, *sources)


def pool_kernel(sizes_ref, offsets_ref, *refs, segments):
    count = sum(len(parts) for parts in segments)
    ins, out, sem = refs[:count], refs[count], refs[count + 1]
    for waiting in (False, True):
        at = 0
        for e, parts in enumerate(segments):
            for a, b in parts:
                ref = ins[at]
                at += 1

                def step(slot, _, ref=ref, a=a, e=e):
                    place = offsets_ref[e] + slot
                    copy = pltpu.make_async_copy(ref.at[slot - a], out.at[place], sem.at[place])
                    if waiting:
                        copy.wait()
                    else:
                        copy.start()
                    return 0

                lax.fori_loop(a, jnp.maximum(a, jnp.minimum(b, sizes_ref[e])), step, 0)


def pool(sizes, offsets, pieces, capacity):
    arrays = [x for parts in pieces for x, _, _ in parts]
    segments = [[(a, b) for _, a, b in parts] for parts in pieces]
    return pl.pallas_call(
        functools.partial(pool_kernel, segments=segments),
        grid_spec=pltpu.PrefetchScalarGridSpec(
            num_scalar_prefetch=2,
            grid=(1,),
            in_specs=[pl.BlockSpec(memory_space=pl.ANY)] * len(arrays),
            out_specs=pl.BlockSpec(memory_space=pl.ANY),
            scratch_shapes=[pltpu.SemaphoreType.DMA((capacity,))],
        ),
        out_shape=jax.ShapeDtypeStruct((capacity, TILE, TILE), jnp.float32),
        compiler_params=pltpu.CompilerParams(vmem_limit_bytes=VMEM_LIMIT),
        cost_estimate=pl.CostEstimate(flops=0, bytes_accessed=8 * capacity * TILE * TILE, transcendentals=0),
    )(sizes, offsets, *arrays)


def gate_kernel(*refs):
    del refs


def gate(released, awaited):
    anywhere = pl.BlockSpec(memory_space=pl.ANY)
    return pl.pallas_call(
        gate_kernel,
        in_specs=[anywhere] * (len(released) + len(awaited)),
        out_specs=[anywhere] * len(released),
        out_shape=[jax.ShapeDtypeStruct(x.shape, x.dtype) for x in released],
        input_output_aliases={i: i for i in range(len(released))},
    )(*released, *awaited)


def multiply_kernel(
    plane_ref, low_ref, high_ref, shift_ref, base_ref, mine_at, other_at, kk_ref, amp_ref, mine_in, other_in, *refs,
    segments, passed, steps, per_chip,
):
    count = len(segments)
    tiles = refs[:count]
    refs = refs[count + passed :]
    mine_ref, other_ref = refs[:2]
    buffer, sem = refs[2 + passed :]
    step = pl.program_id(0)
    rows = mine_ref.shape[0]

    def issue(g, half):
        low, high = low_ref[g], high_ref[g]
        for ref, (a, b, pooled, only) in zip(tiles, segments):
            shift = shift_ref[g] if pooled else -a

            def start(slot, _, ref=ref, shift=shift):
                pltpu.make_async_copy(
                    ref.at[slot + shift], buffer.at[half, slot - low], sem.at[half, slot - low]
                ).start()
                return 0

            first = jnp.maximum(low, a)
            last = jnp.maximum(first, jnp.minimum(high, b))
            if only is not None:
                last = jnp.where(g // per_chip == only, last, first)
            lax.fori_loop(first, last, start, 0)

    half = lax.rem(step, 2)

    @pl.when(step == 0)
    def _():
        issue(0, 0)

    @pl.when(step + 1 < steps)
    def _():
        issue(step + 1, 1 - half)

    mine_ref[...] = mine_in[...]
    other_ref[...] = other_in[...]
    low = low_ref[step]
    length = high_ref[step] - low
    base = base_ref[step] + low

    def wait(at, _):
        pltpu.make_async_copy(tiles[0].at[0], buffer.at[half, at], sem.at[half, at]).wait()
        return 0

    lax.fori_loop(0, length, wait, 0)

    def add(turn, _):
        weights, ks = [], []
        for u in range(UNROLL):
            at = turn * UNROLL + u
            inside = at < length
            at = jnp.minimum(at, length - 1)
            value = buffer[half, at]
            if u:
                value = jnp.where(inside, value, 0.0)
            high = value.astype(jnp.bfloat16)
            rest = (value - high.astype(jnp.float32)).astype(jnp.bfloat16)
            weights.append(jnp.concatenate([high, rest], axis=1))
            weights.append(jnp.concatenate([high, jnp.zeros_like(high)], axis=1))
            ks.append(kk_ref[base + at])
        left = jnp.concatenate([amp_ref[k] for k in ks], axis=1)
        product = jnp.dot(left, jnp.concatenate(weights, axis=0), preferred_element_type=jnp.float32)
        total = product[:, :TILE] + product[:, TILE:]
        mine_ref[...] += total[:rows]
        other_ref[...] += total[rows:]
        return 0

    lax.fori_loop(0, (length + UNROLL - 1) // UNROLL, add, 0)


def multiply(scalars, steps, per_chip, amps, mine, other, pieces, kd, released=()):
    rows = mine.shape[0]
    segments = [piece[1:] for piece in pieces]
    expected = 10 * steps
    n = len(scalars)
    mine_spec = pl.BlockSpec((rows, TILE), lambda g, *s: (0, s[5][g]))
    other_spec = pl.BlockSpec((rows, TILE), lambda g, *s: (0, s[6][g]))
    anywhere = pl.BlockSpec(memory_space=pl.ANY)
    first = n + 3 + len(pieces)
    aliases = {n + 1: 0, n + 2: 1}
    aliases.update({first + i: 2 + i for i in range(len(released))})
    return pl.pallas_call(
        functools.partial(multiply_kernel, segments=segments, passed=len(released), steps=steps, per_chip=per_chip),
        grid_spec=pltpu.PrefetchScalarGridSpec(
            num_scalar_prefetch=n,
            grid=(steps,),
            in_specs=[
                pl.BlockSpec((CORES * kd, CORES * rows, 2 * TILE), lambda g, *s: (s[0][0], 0, 0)),
                mine_spec,
                other_spec,
            ]
            + [anywhere] * (len(pieces) + len(released)),
            out_specs=[mine_spec, other_spec] + [anywhere] * len(released),
            scratch_shapes=[
                pltpu.VMEM((2, CORES * kd, TILE, TILE), jnp.float32),
                pltpu.SemaphoreType.DMA((2, CORES * kd)),
            ],
        ),
        out_shape=[jax.ShapeDtypeStruct(x.shape, x.dtype) for x in (mine, other, *released)],
        input_output_aliases=aliases,
        compiler_params=pltpu.CompilerParams(vmem_limit_bytes=VMEM_LIMIT),
        cost_estimate=pl.CostEstimate(
            flops=expected * 32 * rows * TILE * TILE,
            bytes_accessed=expected * 4 * TILE * TILE,
            transcendentals=0,
        ),
    )(*scalars, amps, mine, other, *[piece[0] for piece in pieces], *released)


def place_kernel(at_ref, mine_in, piece_ref, out_ref):
    out_ref[...] = mine_in[...] + piece_ref[...]


def place(at, mine, piece):
    rows = mine.shape[0]
    spec = pl.BlockSpec((rows, TILE), lambda g, a: (0, a[g]))
    return pl.pallas_call(
        place_kernel,
        grid_spec=pltpu.PrefetchScalarGridSpec(
            num_scalar_prefetch=1,
            grid=(at.shape[0],),
            in_specs=[spec, pl.BlockSpec((rows, TILE), lambda g, a: (0, g))],
            out_specs=spec,
        ),
        out_shape=jax.ShapeDtypeStruct(mine.shape, mine.dtype),
        input_output_aliases={1: 0},
        compiler_params=pltpu.CompilerParams(vmem_limit_bytes=VMEM_LIMIT),
        cost_estimate=pl.CostEstimate(flops=piece.size, bytes_accessed=12 * piece.size, transcendentals=0),
    )(at, mine, piece)


def body(amplitudes, integrals, amp_pattern, int_pattern, *, chips, devices):
    R, Z = chips, devices // CORES
    first, second, depth = amplitudes.shape
    rows = first * second
    kd = integrals.shape[0] // TILE
    ntl = integrals.shape[1] // TILE
    groups = R if ntl % R == 0 else 1
    width = ntl // groups
    per_chip = -(-ntl // CORES)
    tiles = per_chip * CORES * kd

    r = lax.axis_index("row")
    col = lax.axis_index("col")
    core = lax.rem(col, CORES)
    ring = [0] + list(range(1, Z, 2)) + [z for z in range(Z - 1, 0, -1) if z % 2 == 0]
    spot = [ring.index(z) for z in range(Z)]

    def by_row(x, distance):
        return lax.ppermute(x, "row", [(a, a ^ distance) for a in range(R)])

    def by_core(x):
        return lax.ppermute(x, "col", [(a, a ^ 1) for a in range(Z * CORES)])

    def by_plane(x):
        return lax.ppermute(
            x,
            "col",
            [(ring[a] * CORES + c, ring[(a + 1) % Z] * CORES + c) for a in range(Z) for c in range(CORES)],
        )

    blocks = R * ntl
    spare = per_chip * CORES - ntl
    mine = jnp.zeros((rows, (blocks + spare) * TILE), jnp.float32)
    parts_of = [[0], [1, 2], [3]] if R == 4 else [list(range(R))]
    others = [jnp.zeros((rows, len(part) * per_chip * TILE), jnp.float32) for part in parts_of]
    shares = [integrals[:, d * width * TILE : (d + 1) * width * TILE] for d in range(groups)]
    if groups > 1:
        (int_pattern,) = gate([int_pattern], shares[1:])
        amp_pattern, mine, *others = gate([amp_pattern, mine, *others], [])
    for d in range(1, groups):
        shares[d] = by_row(shares[d], d)

    amps_mine = amplitudes.reshape(rows, depth)
    amps = split_amplitudes(amps_mine, by_core(amps_mine), amp_pattern, by_core(amp_pattern), second)
    if groups > 1:
        *shares[1:], mine = gate([*shares[1:], mine], [amps])
    twins = [by_core(x) for x in shares]

    patterns = [int_pattern] + [by_row(int_pattern, d) for d in range(1, R)]
    by_distance = jnp.stack(patterns).reshape(R, Z, CORES * kd, groups, width)
    near = []
    for e in range(R):
        picked = jnp.stack([by_distance[e ^ d, :, :, d] for d in range(groups)], axis=2)
        near.append(picked.reshape(Z, CORES * kd, ntl))
    present = (jnp.stack(near, axis=1) != 0).astype(jnp.int32)
    present = jnp.pad(present, ((0, 0), (0, 0), (0, 0), (0, per_chip * CORES - ntl)))
    present = present.reshape(Z, R, CORES * kd, per_chip, CORES).transpose(0, 1, 4, 3, 2)
    both = present.reshape(Z, R, CORES, tiles)
    cores_counts = jnp.sum(both, axis=-1)
    own = jnp.where(core == 0, both[:, :, 0], both[:, :, 1])
    here = jnp.asarray(spot)[col // CORES]
    planes = jnp.asarray(ring)[lax.rem(here - jnp.arange(Z) + Z, Z)]
    if R == 4:
        own = jnp.stack(
            [
                own[:, 0],
                jnp.where(core == 0, own[:, 1], own[:, 2]),
                jnp.where(core == 0, own[:, 2], own[:, 1]),
                own[:, 3],
            ],
            axis=1,
        )
    own = own[planes]
    counts = jnp.sum(own, axis=-1)
    ids = jnp.arange(tiles)
    slot_of = jnp.sum(own[..., None, :] * (ids[None, :] < ids[:, None]), axis=-1)
    slots = (
        jnp.sum(
            (ids + 1)[None, None, None, :]
            * ((slot_of[:, :, None, :] == ids[:, None]) & (own[:, :, None, :] > 0)),
            axis=-1,
        )
        - 1
    )
    ends = jnp.sum(own[:, :, None, :] * (ids[None, :] < (jnp.arange(per_chip + 1) * CORES * kd)[:, None]), axis=-1)

    straight = max(2, round(tiles * 35 / 72)) if R == 4 else max(4, 2 * round(tiles * 25 / 72))
    extra = max(2, round(tiles * 16 / 72)) if R == 4 else 0
    pooled = max(R, round(tiles * 32 / 72)) if R == 4 else 0
    longest = tiles + straight + extra
    slots = jnp.pad(slots, ((0, 0), (0, 0), (0, longest - tiles)), constant_values=-1)
    most = jnp.max(cores_counts)

    def chips_of(which):
        return r ^ (jnp.stack([0 * which, 1 + which, 2 - which, 0 * which + 3]) if R == 4 else jnp.arange(R))

    chip_of = chips_of(core)

    def columns_of(which):
        column = jnp.arange(per_chip)[None, :] * CORES + which
        group = column // width
        chip = chips_of(which)[:, None]
        at = (((chip ^ group) if groups > 1 else chip) * groups + group) * width + column % width
        return jnp.where(column < ntl, at, blocks).astype(jnp.int32)

    mine_at = columns_of(core)
    received_at = columns_of(1 - core)

    def across(x, near):
        return lax.ppermute(
            x,
            ("row", "col"),
            [
                (a * devices + d, (a ^ (near if d % CORES == 0 else 3 - near)) * devices + d)
                for a in range(R)
                for d in range(devices)
            ],
        )

    def one_round(state, others):
        base, mine = state
        others = list(others)
        after = base + straight
        left = jnp.clip(cores_counts - after, 0, extra)
        fits = jnp.max(jnp.sum(left, axis=1)) <= pooled
        taken = jnp.where(fits, extra, pooled // R) if extra else jnp.int32(0)
        sizes = jnp.clip(counts - after, 0, taken)
        before = chip_of[None, :] < chip_of[:, None]
        offsets = jnp.sum(sizes[:, None, :] * before[None], axis=-1).astype(jnp.int32)
        now = lax.dynamic_slice_in_dim(slots, base, straight + extra, axis=2)
        kk = jnp.maximum(now, 0) % (CORES * kd)
        bounds = jnp.clip(ends - base, 0, straight + taken).astype(jnp.int32)

        column = now[0, 0] // (CORES * kd) * CORES + core
        holder = kk[0, 0] // kd
        source = jnp.where(now[0, 0] < 0, -1, (holder != core) * groups + column // width)
        where = [source, kk[0, 0] % kd * TILE, column % width * TILE]
        plan = ((0, straight), (straight, extra)) if extra else ((0, straight),)
        packed = pack([x.astype(jnp.int32) for x in where], shares + twins, plan)


        def add(mine, other, step, neighbours, low_slot, high_slot, pieces, spot=0):
            low, high, shift, base_at = [], [], [], []
            for e in neighbours:
                limits = jnp.clip(bounds[step, e], low_slot, high_slot)
                low.append(limits[:-1])
                high.append(limits[1:])
                shift.append(jnp.broadcast_to(offsets[step, e] - straight, (per_chip,)))
                base_at.append(jnp.full((per_chip,), (e - neighbours[0]) * (straight + extra)))
            first_e, last_e = neighbours[0], neighbours[-1] + 1
            lists = [jnp.concatenate(x) for x in (low, high, shift, base_at)]
            lists.append(mine_at[first_e:last_e].reshape(-1))
            steps = len(neighbours) * per_chip
            lists.append(jnp.arange(steps) + spot * per_chip)
            scalars = [planes[step].reshape(1), *lists, kk[step, first_e:last_e].reshape(-1)]
            scalars = [x.astype(jnp.int32) for x in scalars]
            return multiply(scalars, steps, per_chip, amps, mine, other, pieces, kd)

        if R == 4:
            end = straight + extra
            sent, late = packed
            along = [sent, by_plane(sent)]
            first_late, second_late = across(late, 1), across(late, 2)
            at_home = [(sent, 0, straight, False, None), (late, straight, end, False, None)]
            mine, others[0] = add(mine, others[0], 0, [0], 0, end, at_home)
            first_late, mine = gate([first_late, mine], [])
            third_late = across(first_late, 2)
            pools = [
                pool(
                    sizes[0].astype(jnp.int32),
                    offsets[0],
                    [[(x, 0, extra)] for x in (late, first_late, second_late, third_late)],
                    pooled,
                )
            ]
            pools.append(by_plane(pools[0]))
            (ready,) = gate([sent], [pools[0]])
            first_near, second_near = across(ready, 1), across(ready, 2)
            received = []
            for step in range(Z):
                first_near, mine = gate([first_near, mine], [second_near])
                third_near = across(first_near, 2)
                mixed = (pools[step], straight, end, True, None)
                near = [(first_near, 0, straight, False, 0), (second_near, 0, straight, False, 1), mixed]
                last = [(third_near, 0, straight, False, None), mixed]
                if step:
                    home = [(along[step], 0, straight, False, None), mixed]
                    mine, others[0] = add(mine, others[0], step, [0], 0, end, home)
                if step == Z - 1:
                    received.append(by_core(others[0]))
                else:
                    along[step + 1], mine = gate([along[step + 1], mine], [third_near])
                    first_near, second_near = across(along[step + 1], 1), across(along[step + 1], 2)
                    if step + 2 < Z:
                        along.append(by_plane(along[step + 1]))
                        pools.append(by_plane(pools[step + 1]))
                mine, others[1] = add(mine, others[1], step, [1, 2], 0, end, near)
                if step == Z - 1:
                    received.append(by_core(others[1]))
                    mine = place(received_at[0], mine, received[0])
                mine, others[2] = add(mine, others[2], step, [3], 0, end, last)
            received.append(by_core(others[2]))
            mine = place(received_at[1:3].reshape(-1), mine, received[1])
            mine = place(received_at[3], mine, received[2])
        else:
            now_at = packed[0]
            for step in range(Z):
                for e in range(R):
                    piece = by_row(now_at, e) if e else now_at
                    mine, others[0] = add(mine, others[0], step, [e], 0, straight, [(piece, 0, straight, False, None)], e)
                if step + 1 < Z:
                    now_at = by_plane(now_at)
            mine = place(received_at.reshape(-1), mine, by_core(others[0]))
        return base + straight + taken, mine

    state = one_round((jnp.int32(0), mine), others)
    cleared = [x.shape for x in others]
    _, mine = lax.while_loop(
        lambda state: state[0] < most,
        lambda state: one_round(state, [jnp.zeros(shape, jnp.float32) for shape in cleared]),
        state,
    )
    return mine[:, : blocks * TILE].reshape(first, second, blocks * TILE)


def solution(mesh):
    placed = (P("col", "row", None), P("col", "row"), P("col", None), P(None, "row"))
    return jax.shard_map(
        functools.partial(body, chips=mesh.shape["row"], devices=mesh.shape["col"]),
        mesh=mesh,
        in_specs=placed,
        out_specs=P("col", "row", None),
        check_vma=False,
    )
```

```python
import functools

import jax
import jax.numpy as jnp
from jax import lax
from jax.experimental import pallas as pl
from jax.experimental.pallas import tpu as pltpu
from jax.sharding import PartitionSpec as P

TILE = 128
CORES = 2
UNROLL = 3
VMEM_LIMIT = 48 * 1024 * 1024


def split_kernel(mine_pattern, other_pattern, mine_ref, other_ref, out_ref, *, second):
    k = pl.program_id(0)
    rows = mine_ref.shape[0]
    for half, (pattern, amp_ref) in enumerate(((mine_pattern, mine_ref), (other_pattern, other_ref))):
        for first in range(rows // second):
            value = amp_ref[pl.ds(first * second, second), :] * pattern[first, k].astype(jnp.float32)
            high = value.astype(jnp.bfloat16)
            low = (value - high.astype(jnp.float32)).astype(jnp.bfloat16)
            here = pl.ds(half * rows + first * second, second)
            out_ref[0, here, :TILE] = high
            out_ref[0, here, TILE:] = low


def split_amplitudes(mine, other, mine_pattern, other_pattern, second):
    rows, depth = mine.shape
    tiles = depth // TILE
    return pl.pallas_call(
        functools.partial(split_kernel, second=second),
        grid_spec=pltpu.PrefetchScalarGridSpec(
            num_scalar_prefetch=2,
            grid=(tiles,),
            in_specs=[pl.BlockSpec((rows, TILE), lambda k, *_: (0, k))] * 2,
            out_specs=pl.BlockSpec((1, CORES * rows, 2 * TILE), lambda k, *_: (k, 0, 0)),
        ),
        out_shape=jax.ShapeDtypeStruct((tiles, CORES * rows, 2 * TILE), jnp.bfloat16),
        compiler_params=pltpu.CompilerParams(vmem_limit_bytes=VMEM_LIMIT),
        cost_estimate=pl.CostEstimate(flops=8 * rows * depth, bytes_accessed=16 * rows * depth, transcendentals=0),
    )(mine_pattern, other_pattern, mine, other)


def pack_kernel(source_ref, row_ref, lane_ref, *refs, plan, sources):
    ins, outs = refs[:sources], refs[sources:]
    for out, (base, size) in zip(outs, plan):

        def copy(slot, _, out=out, base=base):
            row = pl.multiple_of(row_ref[base + slot], TILE)
            lane = pl.multiple_of(lane_ref[base + slot], TILE)
            for source in range(sources):

                @pl.when(source_ref[base + slot] == source)
                def _(source=source):
                    out[slot] = ins[source][pl.ds(row, TILE), pl.ds(lane, TILE)]

            return 0

        lax.fori_loop(0, size, copy, 0)


def pack(scalars, sources, plan):
    whole = lambda x: pl.BlockSpec(x.shape, lambda g, *s: (0,) * len(x.shape))
    outs = [jax.ShapeDtypeStruct((size, TILE, TILE), jnp.float32) for _, size in plan]
    return pl.pallas_call(
        functools.partial(pack_kernel, plan=plan, sources=len(sources)),
        grid_spec=pltpu.PrefetchScalarGridSpec(
            num_scalar_prefetch=len(scalars),
            grid=(1,),
            in_specs=[whole(x) for x in sources],
            out_specs=[whole(x) for x in outs],
        ),
        out_shape=outs,
        compiler_params=pltpu.CompilerParams(vmem_limit_bytes=VMEM_LIMIT),
        cost_estimate=pl.CostEstimate(
            flops=0, bytes_accessed=4 * (sum(x.size for x in sources) + sum(x.size for x in outs)), transcendentals=0
        ),
    )(*scalars, *sources)


def pool_kernel(sizes_ref, offsets_ref, *refs):
    *ins, out = refs
    for e, ref in enumerate(ins):

        def copy(slot, _, ref=ref, e=e):
            out[offsets_ref[e] + slot] = ref[slot]
            return 0

        lax.fori_loop(0, sizes_ref[e], copy, 0)


def pool(sizes, offsets, lists, capacity):
    whole = lambda shape: pl.BlockSpec(shape, lambda g, *s: (0,) * len(shape))
    shape = (capacity, TILE, TILE)
    return pl.pallas_call(
        pool_kernel,
        grid_spec=pltpu.PrefetchScalarGridSpec(
            num_scalar_prefetch=2,
            grid=(1,),
            in_specs=[whole(x.shape) for x in lists],
            out_specs=whole(shape),
        ),
        out_shape=jax.ShapeDtypeStruct(shape, jnp.float32),
        compiler_params=pltpu.CompilerParams(vmem_limit_bytes=VMEM_LIMIT),
        cost_estimate=pl.CostEstimate(flops=0, bytes_accessed=12 * capacity * TILE * TILE, transcendentals=0),
    )(sizes, offsets, *lists)


def gate_kernel(*refs):
    del refs


def gate(released, awaited):
    anywhere = pl.BlockSpec(memory_space=pl.ANY)
    return pl.pallas_call(
        gate_kernel,
        in_specs=[anywhere] * (len(released) + len(awaited)),
        out_specs=[anywhere] * len(released),
        out_shape=[jax.ShapeDtypeStruct(x.shape, x.dtype) for x in released],
        input_output_aliases={i: i for i in range(len(released))},
    )(*released, *awaited)


def multiply_kernel(
    plane_ref, low_ref, high_ref, shift_ref, base_ref, mine_at, other_at, kk_ref, amp_ref, mine_in, other_in, *refs,
    segments, steps, per_chip, wide,
):
    count = len(segments)
    tiles = refs[:count]
    mine_ref, other_ref, buffer, sem = refs[count:]
    step = pl.program_id(0)
    rows = mine_ref.shape[0]

    def issue(g, half):
        low, high = low_ref[g * wide], high_ref[g * wide + wide - 1]
        for ref, (a, b, pooled, only) in zip(tiles, segments):
            shift = shift_ref[g * wide] if pooled else -a

            def start(slot, _, ref=ref, shift=shift):
                pltpu.make_async_copy(
                    ref.at[slot + shift], buffer.at[half, slot - low], sem.at[half, slot - low]
                ).start()
                return 0

            first = jnp.maximum(low, a)
            last = jnp.maximum(first, jnp.minimum(high, b))
            if only is not None:
                last = jnp.where(g * wide // per_chip == only, last, first)
            lax.fori_loop(first, last, start, 0)

    half = lax.rem(step, 2)

    @pl.when(step == 0)
    def _():
        issue(0, 0)

    @pl.when(step + 1 < steps)
    def _():
        issue(step + 1, 1 - half)

    mine_ref[...] = mine_in[...]
    other_ref[...] = other_in[...]
    origin = low_ref[step * wide]
    for i in range(wide):
        lanes = pl.ds(i * TILE, TILE)
        low = low_ref[step * wide + i]
        length = high_ref[step * wide + i] - low
        base = base_ref[step * wide] + low

        def wait(at, _, low=low):
            at = low - origin + at
            pltpu.make_async_copy(tiles[0].at[0], buffer.at[half, at], sem.at[half, at]).wait()
            return 0

        lax.fori_loop(0, length, wait, 0)

        def add(turn, _, lanes=lanes, low=low, length=length, base=base):
            weights, ks = [], []
            for u in range(UNROLL):
                at = turn * UNROLL + u
                inside = at < length
                at = jnp.minimum(at, length - 1)
                value = buffer[half, low - origin + at]
                if u:
                    value = jnp.where(inside, value, 0.0)
                high = value.astype(jnp.bfloat16)
                rest = (value - high.astype(jnp.float32)).astype(jnp.bfloat16)
                weights.append(jnp.concatenate([high, rest], axis=1))
                weights.append(jnp.concatenate([high, jnp.zeros_like(high)], axis=1))
                ks.append(kk_ref[base + at])
            left = jnp.concatenate([amp_ref[k] for k in ks], axis=1)
            product = jnp.dot(left, jnp.concatenate(weights, axis=0), preferred_element_type=jnp.float32)
            total = product[:, :TILE] + product[:, TILE:]
            mine_ref[:, lanes] += total[:rows]
            other_ref[:, lanes] += total[rows:]
            return 0

        lax.fori_loop(0, (length + UNROLL - 1) // UNROLL, add, 0)


def multiply(scalars, steps, per_chip, wide, amps, mine, other, pieces, kd):
    rows = mine.shape[0]
    segments = [piece[1:] for piece in pieces]
    expected = 10 * steps * wide
    n = len(scalars)
    mine_spec = pl.BlockSpec((rows, wide * TILE), lambda g, *s: (0, s[5][g]))
    other_spec = pl.BlockSpec((rows, wide * TILE), lambda g, *s: (0, s[6][g]))
    anywhere = pl.BlockSpec(memory_space=pl.ANY)
    held = CORES * kd * wide
    return pl.pallas_call(
        functools.partial(multiply_kernel, segments=segments, steps=steps, per_chip=per_chip, wide=wide),
        grid_spec=pltpu.PrefetchScalarGridSpec(
            num_scalar_prefetch=n,
            grid=(steps,),
            in_specs=[
                pl.BlockSpec((CORES * kd, CORES * rows, 2 * TILE), lambda g, *s: (s[0][0], 0, 0)),
                mine_spec,
                other_spec,
            ]
            + [anywhere] * len(pieces),
            out_specs=[mine_spec, other_spec],
            scratch_shapes=[pltpu.VMEM((2, held, TILE, TILE), jnp.float32), pltpu.SemaphoreType.DMA((2, held))],
        ),
        out_shape=[jax.ShapeDtypeStruct(x.shape, x.dtype) for x in (mine, other)],
        input_output_aliases={n + 1: 0, n + 2: 1},
        compiler_params=pltpu.CompilerParams(vmem_limit_bytes=VMEM_LIMIT),
        cost_estimate=pl.CostEstimate(
            flops=expected * 32 * rows * TILE * TILE,
            bytes_accessed=expected * 4 * TILE * TILE,
            transcendentals=0,
        ),
    )(*scalars, amps, mine, other, *[piece[0] for piece in pieces])


def place_kernel(at_ref, mine_in, piece_ref, out_ref):
    out_ref[...] = mine_in[...] + piece_ref[...]


def place(at, wide, mine, piece):
    rows = mine.shape[0]
    spec = pl.BlockSpec((rows, wide * TILE), lambda g, a: (0, a[g]))
    return pl.pallas_call(
        place_kernel,
        grid_spec=pltpu.PrefetchScalarGridSpec(
            num_scalar_prefetch=1,
            grid=(at.shape[0],),
            in_specs=[spec, pl.BlockSpec((rows, wide * TILE), lambda g, a: (0, g))],
            out_specs=spec,
        ),
        out_shape=jax.ShapeDtypeStruct(mine.shape, mine.dtype),
        input_output_aliases={1: 0},
        compiler_params=pltpu.CompilerParams(vmem_limit_bytes=VMEM_LIMIT),
        cost_estimate=pl.CostEstimate(flops=piece.size, bytes_accessed=12 * piece.size, transcendentals=0),
    )(at, mine, piece)


def body(amplitudes, integrals, amp_pattern, int_pattern, *, chips, devices):
    R, Z = chips, devices // CORES
    first, second, depth = amplitudes.shape
    rows = first * second
    kd = integrals.shape[0] // TILE
    ntl = integrals.shape[1] // TILE
    groups = R if ntl % R == 0 else 1
    width = ntl // groups
    if groups == 4:
        wide = width
        owned = [[d * width + i for d in pair for i in range(width)] for pair in ((0, 3), (1, 2))]
    else:
        wide = 1
        owned = [list(range(c, ntl, CORES)) for c in range(CORES)]
        owned = [x + [ntl] * (len(owned[0]) - len(x)) for x in owned]
    per_chip = len(owned[0])
    tiles = per_chip * CORES * kd

    r = lax.axis_index("row")
    col = lax.axis_index("col")
    core = lax.rem(col, CORES)
    ring = [0] + list(range(1, Z, 2)) + [z for z in range(Z - 1, 0, -1) if z % 2 == 0]
    spot = [ring.index(z) for z in range(Z)]

    def by_row(x, distance):
        return lax.ppermute(x, "row", [(a, a ^ distance) for a in range(R)])

    def by_core(x):
        return lax.ppermute(x, "col", [(a, a ^ 1) for a in range(Z * CORES)])

    def by_plane(x):
        return lax.ppermute(
            x,
            "col",
            [(ring[a] * CORES + c, ring[(a + 1) % Z] * CORES + c) for a in range(Z) for c in range(CORES)],
        )

    blocks = R * ntl
    spare = per_chip * CORES - ntl
    mine = jnp.zeros((rows, (blocks + spare) * TILE), jnp.float32)
    parts_of = [[0], [1, 2], [3]] if R == 4 else [list(range(R))]
    others = [jnp.zeros((rows, len(part) * per_chip * TILE), jnp.float32) for part in parts_of]
    shares = [integrals[:, d * width * TILE : (d + 1) * width * TILE] for d in range(groups)]
    if groups > 1:
        (int_pattern,) = gate([int_pattern], shares[1:])
        amp_pattern, mine, *others = gate([amp_pattern, mine, *others], [])
    for d in range(1, groups):
        shares[d] = by_row(shares[d], d)

    amps_mine = amplitudes.reshape(rows, depth)
    amps = split_amplitudes(amps_mine, by_core(amps_mine), amp_pattern, by_core(amp_pattern), second)
    if groups > 1:
        *shares[1:], mine = gate([*shares[1:], mine], [amps])
    twins = [by_core(x) for x in shares]

    patterns = [int_pattern] + [by_row(int_pattern, d) for d in range(1, R)]
    by_distance = jnp.stack(patterns).reshape(R, Z, CORES * kd, groups, width)
    near = []
    for e in range(R):
        picked = jnp.stack([by_distance[e ^ d, :, :, d] for d in range(groups)], axis=2)
        near.append(picked.reshape(Z, CORES * kd, ntl))
    present = (jnp.stack(near, axis=1) != 0).astype(jnp.int32)
    present = jnp.pad(present, ((0, 0), (0, 0), (0, 0), (0, per_chip * CORES - ntl)))
    present = jnp.stack([jnp.stack([present[..., j] for j in x], axis=-1) for x in owned], axis=-1)
    present = present.transpose(0, 1, 4, 3, 2)
    both = present.reshape(Z, R, CORES, tiles)
    cores_counts = jnp.sum(both, axis=-1)
    own = jnp.where(core == 0, both[:, :, 0], both[:, :, 1])
    here = jnp.asarray(spot)[col // CORES]
    planes = jnp.asarray(ring)[lax.rem(here - jnp.arange(Z) + Z, Z)]
    if R == 4:
        own = jnp.stack(
            [
                own[:, 0],
                jnp.where(core == 0, own[:, 1], own[:, 2]),
                jnp.where(core == 0, own[:, 2], own[:, 1]),
                own[:, 3],
            ],
            axis=1,
        )
    own = own[planes]
    counts = jnp.sum(own, axis=-1)
    ids = jnp.arange(tiles)
    slot_of = jnp.sum(own[..., None, :] * (ids[None, :] < ids[:, None]), axis=-1)
    slots = (
        jnp.sum(
            (ids + 1)[None, None, None, :]
            * ((slot_of[:, :, None, :] == ids[:, None]) & (own[:, :, None, :] > 0)),
            axis=-1,
        )
        - 1
    )
    ends = jnp.sum(own[:, :, None, :] * (ids[None, :] < (jnp.arange(per_chip + 1) * CORES * kd)[:, None]), axis=-1)

    straight = max(2, round(tiles * 35 / 72)) if R == 4 else max(4, 2 * round(tiles * 25 / 72))
    extra = max(2, round(tiles * 16 / 72)) if R == 4 else 0
    pooled = max(R, round(tiles * 32 / 72)) if R == 4 else 0
    longest = tiles + straight + extra
    slots = jnp.pad(slots, ((0, 0), (0, 0), (0, longest - tiles)), constant_values=-1)
    most = jnp.max(cores_counts)

    def chips_of(which):
        return r ^ (jnp.stack([0 * which, 1 + which, 2 - which, 0 * which + 3]) if R == 4 else jnp.arange(R))

    chip_of = chips_of(core)

    def columns_of(which):
        column = jnp.asarray(owned)[which][None, ::wide]
        group = column // width
        chip = chips_of(which)[:, None]
        at = (((chip ^ group) if groups > 1 else chip) * groups + group) * width + column % width
        return (jnp.where(column < ntl, at, blocks) // wide).astype(jnp.int32)

    mine_at = columns_of(core)
    received_at = columns_of(1 - core)

    def across(x, near):
        return lax.ppermute(
            x,
            ("row", "col"),
            [
                (a * devices + d, (a ^ (near if d % CORES == 0 else 3 - near)) * devices + d)
                for a in range(R)
                for d in range(devices)
            ],
        )

    def one_round(state, others):
        base, mine = state
        others = list(others)
        after = base + straight
        left = jnp.clip(cores_counts - after, 0, extra)
        fits = jnp.max(jnp.sum(left, axis=1)) <= pooled
        taken = jnp.where(fits, extra, pooled // R) if extra else jnp.int32(0)
        sizes = jnp.clip(counts - after, 0, taken)
        before = chip_of[None, :] < chip_of[:, None]
        offsets = jnp.sum(sizes[:, None, :] * before[None], axis=-1).astype(jnp.int32)
        now = lax.dynamic_slice_in_dim(slots, base, straight + extra, axis=2)
        kk = jnp.maximum(now, 0) % (CORES * kd)
        bounds = jnp.clip(ends - base, 0, straight + taken).astype(jnp.int32)

        column = jnp.asarray(owned)[core][jnp.maximum(now[0, 0], 0) // (CORES * kd)]
        holder = kk[0, 0] // kd
        source = jnp.where(now[0, 0] < 0, -1, (holder != core) * groups + column // width)
        where = [source, kk[0, 0] % kd * TILE, column % width * TILE]
        plan = ((0, straight), (straight, extra)) if extra else ((0, straight),)
        packed = pack([x.astype(jnp.int32) for x in where], shares + twins, plan)


        def add(mine, other, step, neighbours, low_slot, high_slot, pieces, spot=0):
            low, high, shift, base_at = [], [], [], []
            for e in neighbours:
                limits = jnp.clip(bounds[step, e], low_slot, high_slot)
                low.append(limits[:-1])
                high.append(limits[1:])
                shift.append(jnp.broadcast_to(offsets[step, e] - straight, (per_chip,)))
                base_at.append(jnp.full((per_chip,), (e - neighbours[0]) * (straight + extra)))
            first_e, last_e = neighbours[0], neighbours[-1] + 1
            lists = [jnp.concatenate(x) for x in (low, high, shift, base_at)]
            lists.append(mine_at[first_e:last_e].reshape(-1))
            steps = len(neighbours) * per_chip // wide
            lists.append(jnp.arange(steps) + spot * per_chip // wide)
            scalars = [planes[step].reshape(1), *lists, kk[step, first_e:last_e].reshape(-1)]
            scalars = [x.astype(jnp.int32) for x in scalars]
            return multiply(scalars, steps, per_chip, wide, amps, mine, other, pieces, kd)

        if R == 4:
            end = straight + extra
            sent, late = packed
            along = [sent, by_plane(sent)]
            first_late, second_late = across(late, 1), across(late, 2)
            at_home = [(sent, 0, straight, False, None), (late, straight, end, False, None)]
            mine, others[0] = add(mine, others[0], 0, [0], 0, end, at_home)
            first_late, mine = gate([first_late, mine], [])
            third_late = across(first_late, 2)
            pools = [
                pool(
                    sizes[0].astype(jnp.int32),
                    offsets[0],
                    [late, first_late, second_late, third_late],
                    pooled,
                )
            ]
            pools.append(by_plane(pools[0]))
            (ready,) = gate([sent], [pools[0]])
            first_near, second_near = across(ready, 1), across(ready, 2)
            received = []
            for step in range(Z):
                first_near, mine = gate([first_near, mine], [second_near])
                third_near = across(first_near, 2)
                mixed = (pools[step], straight, end, True, None)
                near = [(first_near, 0, straight, False, 0), (second_near, 0, straight, False, 1), mixed]
                last = [(third_near, 0, straight, False, None), mixed]
                if step:
                    home = [(along[step], 0, straight, False, None), mixed]
                    mine, others[0] = add(mine, others[0], step, [0], 0, end, home)
                if step == Z - 1:
                    received.append(by_core(others[0]))
                else:
                    along[step + 1], mine = gate([along[step + 1], mine], [third_near])
                    first_near, second_near = across(along[step + 1], 1), across(along[step + 1], 2)
                    if step + 2 < Z:
                        along.append(by_plane(along[step + 1]))
                        pools.append(by_plane(pools[step + 1]))
                mine, others[1] = add(mine, others[1], step, [1, 2], 0, end, near)
                if step == Z - 1:
                    received.append(by_core(others[1]))
                    mine = place(received_at[0], wide, mine, received[0])
                mine, others[2] = add(mine, others[2], step, [3], 0, end, last)
            received.append(by_core(others[2]))
            mine = place(received_at[1:3].reshape(-1), wide, mine, received[1])
            mine = place(received_at[3], wide, mine, received[2])
        else:
            now_at = packed[0]
            for step in range(Z):
                for e in range(R):
                    piece = by_row(now_at, e) if e else now_at
                    mine, others[0] = add(mine, others[0], step, [e], 0, straight, [(piece, 0, straight, False, None)], e)
                if step + 1 < Z:
                    now_at = by_plane(now_at)
            mine = place(received_at.reshape(-1), wide, mine, by_core(others[0]))
        return base + straight + taken, mine

    state = one_round((jnp.int32(0), mine), others)
    cleared = [x.shape for x in others]
    _, mine = lax.while_loop(
        lambda state: state[0] < most,
        lambda state: one_round(state, [jnp.zeros(shape, jnp.float32) for shape in cleared]),
        state,
    )
    return mine[:, : blocks * TILE].reshape(first, second, blocks * TILE)


def solution(mesh):
    placed = (P("col", "row", None), P("col", "row"), P("col", None), P(None, "row"))
    return jax.shard_map(
        functools.partial(body, chips=mesh.shape["row"], devices=mesh.shape["col"]),
        mesh=mesh,
        in_specs=placed,
        out_specs=P("col", "row", None),
        check_vma=False,
    )
```

```python
import functools

import jax
import jax.numpy as jnp
from jax import lax
from jax.experimental import pallas as pl
from jax.experimental.pallas import tpu as pltpu
from jax.sharding import PartitionSpec as P

TILE = 128
CORES = 2
UNROLL = 3
VMEM_LIMIT = 48 * 1024 * 1024


def split_kernel(mine_pattern, other_pattern, mine_ref, other_ref, out_ref, *cleared, second, deep):
    rows = mine_ref.shape[0]
    for ref in cleared:
        ref[...] = jnp.zeros_like(ref)
    for i in range(deep):
        k = pl.program_id(0) * deep + i
        lanes = pl.ds(i * TILE, TILE)
        for half, (pattern, amp_ref) in enumerate(((mine_pattern, mine_ref), (other_pattern, other_ref))):
            for first in range(rows // second):
                value = amp_ref[pl.ds(first * second, second), lanes] * pattern[first, k].astype(jnp.float32)
                high = value.astype(jnp.bfloat16)
                low = (value - high.astype(jnp.float32)).astype(jnp.bfloat16)
                here = pl.ds(half * rows + first * second, second)
                out_ref[i, here, :TILE] = high
                out_ref[i, here, TILE:] = low


def split_amplitudes(mine, other, mine_pattern, other_pattern, second, blocks):
    rows, depth = mine.shape
    tiles = depth // TILE
    deep = 4 if tiles % 4 == 0 else 1
    steps = tiles // deep
    out_shape = [jax.ShapeDtypeStruct((tiles, CORES * rows, 2 * TILE), jnp.bfloat16)]
    out_specs = [pl.BlockSpec((deep, CORES * rows, 2 * TILE), lambda k, *_: (k, 0, 0))]
    if blocks % steps == 0:
        out_shape.append(jax.ShapeDtypeStruct((rows, blocks * TILE), jnp.float32))
        out_specs.append(pl.BlockSpec((rows, blocks // steps * TILE), lambda k, *_: (0, k)))
    made = pl.pallas_call(
        functools.partial(split_kernel, second=second, deep=deep),
        grid_spec=pltpu.PrefetchScalarGridSpec(
            num_scalar_prefetch=2,
            grid=(steps,),
            in_specs=[pl.BlockSpec((rows, deep * TILE), lambda k, *_: (0, k))] * 2,
            out_specs=out_specs,
        ),
        out_shape=out_shape,
        compiler_params=pltpu.CompilerParams(vmem_limit_bytes=VMEM_LIMIT),
        cost_estimate=pl.CostEstimate(flops=8 * rows * depth, bytes_accessed=20 * rows * depth, transcendentals=0),
    )(mine_pattern, other_pattern, mine, other)
    return made if len(made) == 2 else (made[0], jnp.zeros((rows, blocks * TILE), jnp.float32))


def pack_kernel(source_ref, row_ref, lane_ref, *refs, plan, sources):
    ins, outs = refs[:sources], refs[sources:]
    for out, (base, size) in zip(outs, plan):

        def copy(slot, _, out=out, base=base):
            row = pl.multiple_of(row_ref[base + slot], TILE)
            lane = pl.multiple_of(lane_ref[base + slot], TILE)
            for source in range(sources):

                @pl.when(source_ref[base + slot] == source)
                def _(source=source):
                    out[slot] = ins[source][pl.ds(row, TILE), pl.ds(lane, TILE)]

            return 0

        lax.fori_loop(0, size, copy, 0)


def pack(scalars, sources, plan):
    whole = lambda x: pl.BlockSpec(x.shape, lambda g, *s: (0,) * len(x.shape))
    outs = [jax.ShapeDtypeStruct((size, TILE, TILE), jnp.float32) for _, size in plan]
    return pl.pallas_call(
        functools.partial(pack_kernel, plan=plan, sources=len(sources)),
        grid_spec=pltpu.PrefetchScalarGridSpec(
            num_scalar_prefetch=len(scalars),
            grid=(1,),
            in_specs=[whole(x) for x in sources],
            out_specs=[whole(x) for x in outs],
        ),
        out_shape=outs,
        compiler_params=pltpu.CompilerParams(vmem_limit_bytes=VMEM_LIMIT),
        cost_estimate=pl.CostEstimate(
            flops=0, bytes_accessed=4 * (sum(x.size for x in sources) + sum(x.size for x in outs)), transcendentals=0
        ),
    )(*scalars, *sources)


def pool_kernel(sizes_ref, offsets_ref, *refs):
    *ins, out = refs
    for e, ref in enumerate(ins):

        def copy(slot, _, ref=ref, e=e):
            out[offsets_ref[e] + slot] = ref[slot]
            return 0

        lax.fori_loop(0, sizes_ref[e], copy, 0)


def pool(sizes, offsets, lists, capacity):
    whole = lambda shape: pl.BlockSpec(shape, lambda g, *s: (0,) * len(shape))
    shape = (capacity, TILE, TILE)
    return pl.pallas_call(
        pool_kernel,
        grid_spec=pltpu.PrefetchScalarGridSpec(
            num_scalar_prefetch=2,
            grid=(1,),
            in_specs=[whole(x.shape) for x in lists],
            out_specs=whole(shape),
        ),
        out_shape=jax.ShapeDtypeStruct(shape, jnp.float32),
        compiler_params=pltpu.CompilerParams(vmem_limit_bytes=VMEM_LIMIT),
        cost_estimate=pl.CostEstimate(flops=0, bytes_accessed=12 * capacity * TILE * TILE, transcendentals=0),
    )(sizes, offsets, *lists)


def gate_kernel(*refs):
    del refs


def gate(released, awaited):
    anywhere = pl.BlockSpec(memory_space=pl.ANY)
    return pl.pallas_call(
        gate_kernel,
        in_specs=[anywhere] * (len(released) + len(awaited)),
        out_specs=[anywhere] * len(released),
        out_shape=[jax.ShapeDtypeStruct(x.shape, x.dtype) for x in released],
        input_output_aliases={i: i for i in range(len(released))},
    )(*released, *awaited)


def multiply_kernel(
    plane_ref, low_ref, high_ref, shift_ref, base_ref, mine_at, other_at, kk_ref, amp_ref, mine_in, other_in, *refs,
    segments, steps, per_chip, wide,
):
    count = len(segments)
    tiles = refs[:count]
    mine_ref, other_ref, buffer, sem = refs[count:]
    step = pl.program_id(0)
    rows = mine_ref.shape[0]

    def issue(g, half):
        low, high = low_ref[g * wide], high_ref[g * wide + wide - 1]
        for ref, (a, b, pooled, only) in zip(tiles, segments):
            shift = shift_ref[g * wide] if pooled else -a

            def start(slot, _, ref=ref, shift=shift):
                pltpu.make_async_copy(
                    ref.at[slot + shift], buffer.at[half, slot - low], sem.at[half, slot - low]
                ).start()
                return 0

            first = jnp.maximum(low, a)
            last = jnp.maximum(first, jnp.minimum(high, b))
            if only is not None:
                last = jnp.where(g * wide // per_chip == only, last, first)
            lax.fori_loop(first, last, start, 0)

    half = lax.rem(step, 2)

    @pl.when(step == 0)
    def _():
        issue(0, 0)

    @pl.when(step + 1 < steps)
    def _():
        issue(step + 1, 1 - half)

    mine_ref[...] = mine_in[...]
    other_ref[...] = other_in[...]
    origin = low_ref[step * wide]
    for i in range(wide):
        lanes = pl.ds(i * TILE, TILE)
        low = low_ref[step * wide + i]
        length = high_ref[step * wide + i] - low
        base = base_ref[step * wide] + low

        def wait(at, _, low=low):
            at = low - origin + at
            pltpu.make_async_copy(tiles[0].at[0], buffer.at[half, at], sem.at[half, at]).wait()
            return 0

        lax.fori_loop(0, length, wait, 0)

        def add(turn, _, lanes=lanes, low=low, length=length, base=base):
            weights, ks = [], []
            for u in range(UNROLL):
                at = turn * UNROLL + u
                inside = at < length
                at = jnp.minimum(at, length - 1)
                value = buffer[half, low - origin + at]
                if u:
                    value = jnp.where(inside, value, 0.0)
                high = value.astype(jnp.bfloat16)
                rest = (value - high.astype(jnp.float32)).astype(jnp.bfloat16)
                weights.append(jnp.concatenate([high, rest], axis=1))
                weights.append(jnp.concatenate([high, jnp.zeros_like(high)], axis=1))
                ks.append(kk_ref[base + at])
            left = jnp.concatenate([amp_ref[k] for k in ks], axis=1)
            product = jnp.dot(left, jnp.concatenate(weights, axis=0), preferred_element_type=jnp.float32)
            total = product[:, :TILE] + product[:, TILE:]
            mine_ref[:, lanes] += total[:rows]
            other_ref[:, lanes] += total[rows:]
            return 0

        lax.fori_loop(0, (length + UNROLL - 1) // UNROLL, add, 0)


def multiply(scalars, steps, per_chip, wide, amps, mine, other, pieces, kd):
    rows = mine.shape[0]
    segments = [piece[1:] for piece in pieces]
    expected = 10 * steps * wide
    n = len(scalars)
    mine_spec = pl.BlockSpec((rows, wide * TILE), lambda g, *s: (0, s[5][g]))
    other_spec = pl.BlockSpec((rows, wide * TILE), lambda g, *s: (0, s[6][g]))
    anywhere = pl.BlockSpec(memory_space=pl.ANY)
    held = CORES * kd * wide
    return pl.pallas_call(
        functools.partial(multiply_kernel, segments=segments, steps=steps, per_chip=per_chip, wide=wide),
        grid_spec=pltpu.PrefetchScalarGridSpec(
            num_scalar_prefetch=n,
            grid=(steps,),
            in_specs=[
                pl.BlockSpec((CORES * kd, CORES * rows, 2 * TILE), lambda g, *s: (s[0][0], 0, 0)),
                mine_spec,
                other_spec,
            ]
            + [anywhere] * len(pieces),
            out_specs=[mine_spec, other_spec],
            scratch_shapes=[pltpu.VMEM((2, held, TILE, TILE), jnp.float32), pltpu.SemaphoreType.DMA((2, held))],
        ),
        out_shape=[jax.ShapeDtypeStruct(x.shape, x.dtype) for x in (mine, other)],
        input_output_aliases={n + 1: 0, n + 2: 1},
        compiler_params=pltpu.CompilerParams(vmem_limit_bytes=VMEM_LIMIT),
        cost_estimate=pl.CostEstimate(
            flops=expected * 32 * rows * TILE * TILE,
            bytes_accessed=expected * 4 * TILE * TILE,
            transcendentals=0,
        ),
    )(*scalars, amps, mine, other, *[piece[0] for piece in pieces])


def place_kernel(at_ref, mine_in, piece_ref, out_ref):
    out_ref[...] = mine_in[...] + piece_ref[...]


def place(at, wide, mine, piece):
    rows = mine.shape[0]
    spec = pl.BlockSpec((rows, wide * TILE), lambda g, a: (0, a[g]))
    return pl.pallas_call(
        place_kernel,
        grid_spec=pltpu.PrefetchScalarGridSpec(
            num_scalar_prefetch=1,
            grid=(at.shape[0],),
            in_specs=[spec, pl.BlockSpec((rows, wide * TILE), lambda g, a: (0, g))],
            out_specs=spec,
        ),
        out_shape=jax.ShapeDtypeStruct(mine.shape, mine.dtype),
        input_output_aliases={1: 0},
        compiler_params=pltpu.CompilerParams(vmem_limit_bytes=VMEM_LIMIT),
        cost_estimate=pl.CostEstimate(flops=piece.size, bytes_accessed=12 * piece.size, transcendentals=0),
    )(at, mine, piece)


def body(amplitudes, integrals, amp_pattern, int_pattern, *, chips, devices):
    R, Z = chips, devices // CORES
    first, second, depth = amplitudes.shape
    rows = first * second
    kd = integrals.shape[0] // TILE
    ntl = integrals.shape[1] // TILE
    groups = R if ntl % R == 0 else 1
    width = ntl // groups
    if groups == 4:
        wide = width
        owned = [[d * width + i for d in pair for i in range(width)] for pair in ((0, 3), (1, 2))]
    else:
        wide = 1
        owned = [list(range(c, ntl, CORES)) for c in range(CORES)]
        owned = [x + [ntl] * (len(owned[0]) - len(x)) for x in owned]
    per_chip = len(owned[0])
    tiles = per_chip * CORES * kd

    r = lax.axis_index("row")
    col = lax.axis_index("col")
    core = lax.rem(col, CORES)
    ring = [0] + list(range(1, Z, 2)) + [z for z in range(Z - 1, 0, -1) if z % 2 == 0]
    spot = [ring.index(z) for z in range(Z)]

    def by_row(x, distance):
        return lax.ppermute(x, "row", [(a, a ^ distance) for a in range(R)])

    def by_core(x):
        return lax.ppermute(x, "col", [(a, a ^ 1) for a in range(Z * CORES)])

    def by_plane(x):
        return lax.ppermute(
            x,
            "col",
            [(ring[a] * CORES + c, ring[(a + 1) % Z] * CORES + c) for a in range(Z) for c in range(CORES)],
        )

    blocks = R * ntl
    spare = per_chip * CORES - ntl
    parts_of = [[0], [1, 2], [3]] if R == 4 else [list(range(R))]
    others = [jnp.zeros((rows, len(part) * per_chip * TILE), jnp.float32) for part in parts_of]
    shares = [integrals[:, d * width * TILE : (d + 1) * width * TILE] for d in range(groups)]
    if groups > 1:
        (int_pattern,) = gate([int_pattern], shares[1:])
    for d in range(1, groups):
        shares[d] = by_row(shares[d], d)

    amps_mine = amplitudes.reshape(rows, depth)
    amps, mine = split_amplitudes(
        amps_mine, by_core(amps_mine), amp_pattern, by_core(amp_pattern), second, blocks + spare
    )
    if groups > 1:
        shares[1:] = gate(shares[1:], [amps])
    twins = [by_core(x) for x in shares]

    patterns = [int_pattern] + [by_row(int_pattern, d) for d in range(1, R)]
    by_distance = jnp.stack(patterns).reshape(R, Z, CORES * kd, groups, width)
    near = []
    for e in range(R):
        picked = jnp.stack([by_distance[e ^ d, :, :, d] for d in range(groups)], axis=2)
        near.append(picked.reshape(Z, CORES * kd, ntl))
    present = (jnp.stack(near, axis=1) != 0).astype(jnp.int32)
    present = jnp.pad(present, ((0, 0), (0, 0), (0, 0), (0, per_chip * CORES - ntl)))
    present = jnp.stack([jnp.stack([present[..., j] for j in x], axis=-1) for x in owned], axis=-1)
    present = present.transpose(0, 1, 4, 3, 2)
    both = present.reshape(Z, R, CORES, tiles)
    cores_counts = jnp.sum(both, axis=-1)
    own = jnp.where(core == 0, both[:, :, 0], both[:, :, 1])
    here = jnp.asarray(spot)[col // CORES]
    planes = jnp.asarray(ring)[lax.rem(here - jnp.arange(Z) + Z, Z)]
    if R == 4:
        own = jnp.stack(
            [
                own[:, 0],
                jnp.where(core == 0, own[:, 1], own[:, 2]),
                jnp.where(core == 0, own[:, 2], own[:, 1]),
                own[:, 3],
            ],
            axis=1,
        )
    own = own[planes]
    counts = jnp.sum(own, axis=-1)
    ids = jnp.arange(tiles)
    slot_of = jnp.sum(own[..., None, :] * (ids[None, :] < ids[:, None]), axis=-1)
    slots = (
        jnp.sum(
            (ids + 1)[None, None, None, :]
            * ((slot_of[:, :, None, :] == ids[:, None]) & (own[:, :, None, :] > 0)),
            axis=-1,
        )
        - 1
    )
    ends = jnp.sum(own[:, :, None, :] * (ids[None, :] < (jnp.arange(per_chip + 1) * CORES * kd)[:, None]), axis=-1)

    straight = max(2, round(tiles * 35 / 72)) if R == 4 else max(4, 2 * round(tiles * 25 / 72))
    extra = max(2, round(tiles * 16 / 72)) if R == 4 else 0
    pooled = max(R, round(tiles * 32 / 72)) if R == 4 else 0
    longest = tiles + straight + extra
    slots = jnp.pad(slots, ((0, 0), (0, 0), (0, longest - tiles)), constant_values=-1)
    most = jnp.max(cores_counts)

    def chips_of(which):
        return r ^ (jnp.stack([0 * which, 1 + which, 2 - which, 0 * which + 3]) if R == 4 else jnp.arange(R))

    chip_of = chips_of(core)

    def columns_of(which):
        column = jnp.asarray(owned)[which][None, ::wide]
        group = column // width
        chip = chips_of(which)[:, None]
        at = (((chip ^ group) if groups > 1 else chip) * groups + group) * width + column % width
        return (jnp.where(column < ntl, at, blocks) // wide).astype(jnp.int32)

    mine_at = columns_of(core)
    received_at = columns_of(1 - core)

    def across(x, near):
        return lax.ppermute(
            x,
            ("row", "col"),
            [
                (a * devices + d, (a ^ (near if d % CORES == 0 else 3 - near)) * devices + d)
                for a in range(R)
                for d in range(devices)
            ],
        )

    def one_round(state, others):
        base, mine = state
        others = list(others)
        after = base + straight
        left = jnp.clip(cores_counts - after, 0, extra)
        fits = jnp.max(jnp.sum(left, axis=1)) <= pooled
        taken = jnp.where(fits, extra, pooled // R) if extra else jnp.int32(0)
        sizes = jnp.clip(counts - after, 0, taken)
        before = chip_of[None, :] < chip_of[:, None]
        offsets = jnp.sum(sizes[:, None, :] * before[None], axis=-1).astype(jnp.int32)
        now = lax.dynamic_slice_in_dim(slots, base, straight + extra, axis=2)
        kk = jnp.maximum(now, 0) % (CORES * kd)
        bounds = jnp.clip(ends - base, 0, straight + taken).astype(jnp.int32)

        column = jnp.asarray(owned)[core][jnp.maximum(now[0, 0], 0) // (CORES * kd)]
        holder = kk[0, 0] // kd
        source = jnp.where(now[0, 0] < 0, -1, (holder != core) * groups + column // width)
        where = [source, kk[0, 0] % kd * TILE, column % width * TILE]
        plan = ((0, straight), (straight, extra), (0, straight)) if extra else ((0, straight),)
        packed = pack([x.astype(jnp.int32) for x in where], shares + twins, plan)


        def add(mine, other, step, neighbours, low_slot, high_slot, pieces, spot=0):
            low, high, shift, base_at = [], [], [], []
            for e in neighbours:
                limits = jnp.clip(bounds[step, e], low_slot, high_slot)
                low.append(limits[:-1])
                high.append(limits[1:])
                shift.append(jnp.broadcast_to(offsets[step, e] - straight, (per_chip,)))
                base_at.append(jnp.full((per_chip,), (e - neighbours[0]) * (straight + extra)))
            first_e, last_e = neighbours[0], neighbours[-1] + 1
            lists = [jnp.concatenate(x) for x in (low, high, shift, base_at)]
            lists.append(mine_at[first_e:last_e].reshape(-1))
            steps = len(neighbours) * per_chip // wide
            lists.append(jnp.arange(steps) + spot * per_chip // wide)
            scalars = [planes[step].reshape(1), *lists, kk[step, first_e:last_e].reshape(-1)]
            scalars = [x.astype(jnp.int32) for x in scalars]
            return multiply(scalars, steps, per_chip, wide, amps, mine, other, pieces, kd)

        if R == 4:
            end = straight + extra
            sent, late, ready = packed
            along = [sent, by_plane(sent)]
            first_late, second_late = across(late, 1), across(late, 2)
            at_home = [(sent, 0, straight, False, None), (late, straight, end, False, None)]
            mine, others[0] = add(mine, others[0], 0, [0], 0, end, at_home)
            first_late, ready, mine = gate([first_late, ready, mine], [second_late])
            third_late = across(first_late, 2)
            first_near, second_near = across(ready, 1), across(ready, 2)
            pools = [
                pool(
                    sizes[0].astype(jnp.int32),
                    offsets[0],
                    [late, first_late, second_late, third_late],
                    pooled,
                )
            ]
            pools.append(by_plane(pools[0]))
            received = []
            for step in range(Z):
                first_near, mine = gate([first_near, mine], [second_near, pools[step]])
                third_near = across(first_near, 2)
                mixed = (pools[step], straight, end, True, None)
                near = [(first_near, 0, straight, False, 0), (second_near, 0, straight, False, 1), mixed]
                last = [(third_near, 0, straight, False, None), mixed]
                if step:
                    home = [(along[step], 0, straight, False, None), mixed]
                    mine, others[0] = add(mine, others[0], step, [0], 0, end, home)
                if step == Z - 1:
                    received.append(by_core(others[0]))
                else:
                    along[step + 1], mine = gate([along[step + 1], mine], [third_near])
                    first_near, second_near = across(along[step + 1], 1), across(along[step + 1], 2)
                    if step + 2 < Z:
                        along.append(by_plane(along[step + 1]))
                        pools.append(by_plane(pools[step + 1]))
                mine, others[1] = add(mine, others[1], step, [1, 2], 0, end, near)
                if step == Z - 1:
                    received.append(by_core(others[1]))
                    mine = place(received_at[0], wide, mine, received[0])
                mine, others[2] = add(mine, others[2], step, [3], 0, end, last)
            received.append(by_core(others[2]))
            mine = place(received_at[1:3].reshape(-1), wide, mine, received[1])
            mine = place(received_at[3], wide, mine, received[2])
        else:
            now_at = packed[0]
            for step in range(Z):
                for e in range(R):
                    piece = by_row(now_at, e) if e else now_at
                    mine, others[0] = add(mine, others[0], step, [e], 0, straight, [(piece, 0, straight, False, None)], e)
                if step + 1 < Z:
                    now_at = by_plane(now_at)
            mine = place(received_at.reshape(-1), wide, mine, by_core(others[0]))
        return base + straight + taken, mine

    state = one_round((jnp.int32(0), mine), others)
    cleared = [x.shape for x in others]
    _, mine = lax.while_loop(
        lambda state: state[0] < most,
        lambda state: one_round(state, [jnp.zeros(shape, jnp.float32) for shape in cleared]),
        state,
    )
    return mine[:, : blocks * TILE].reshape(first, second, blocks * TILE)


def solution(mesh):
    placed = (P("col", "row", None), P("col", "row"), P("col", None), P(None, "row"))
    return jax.shard_map(
        functools.partial(body, chips=mesh.shape["row"], devices=mesh.shape["col"]),
        mesh=mesh,
        in_specs=placed,
        out_specs=P("col", "row", None),
        check_vma=False,
    )
```

```python
import functools

import jax
import jax.numpy as jnp
from jax import lax
from jax.experimental import pallas as pl
from jax.experimental.pallas import tpu as pltpu
from jax.sharding import PartitionSpec as P

TILE = 128
CORES = 2
UNROLL = 3
VMEM_LIMIT = 48 * 1024 * 1024


def split_kernel(mine_pattern, other_pattern, mine_ref, other_ref, lists_ref, out_ref, *cleared, second, deep):
    del lists_ref
    rows = mine_ref.shape[0]
    for ref in cleared:
        ref[...] = jnp.zeros_like(ref)
    for i in range(deep):
        k = pl.program_id(0) * deep + i
        lanes = pl.ds(i * TILE, TILE)
        for half, (pattern, amp_ref) in enumerate(((mine_pattern, mine_ref), (other_pattern, other_ref))):
            for first in range(rows // second):
                value = amp_ref[pl.ds(first * second, second), lanes] * pattern[first, k].astype(jnp.float32)
                high = value.astype(jnp.bfloat16)
                low = (value - high.astype(jnp.float32)).astype(jnp.bfloat16)
                here = pl.ds(half * rows + first * second, second)
                out_ref[i, here, :TILE] = high
                out_ref[i, here, TILE:] = low


def split_amplitudes(mine, other, mine_pattern, other_pattern, lists, second, blocks):
    rows, depth = mine.shape
    tiles = depth // TILE
    deep = 4 if tiles % 4 == 0 else 1
    steps = tiles // deep
    out_shape = [jax.ShapeDtypeStruct((tiles, CORES * rows, 2 * TILE), jnp.bfloat16)]
    out_specs = [pl.BlockSpec((deep, CORES * rows, 2 * TILE), lambda k, *_: (k, 0, 0))]
    if blocks % steps == 0:
        out_shape.append(jax.ShapeDtypeStruct((rows, blocks * TILE), jnp.float32))
        out_specs.append(pl.BlockSpec((rows, blocks // steps * TILE), lambda k, *_: (0, k)))
    made = pl.pallas_call(
        functools.partial(split_kernel, second=second, deep=deep),
        grid_spec=pltpu.PrefetchScalarGridSpec(
            num_scalar_prefetch=2,
            grid=(steps,),
            in_specs=[pl.BlockSpec((rows, deep * TILE), lambda k, *_: (0, k))] * 2 + [pl.BlockSpec(memory_space=pl.ANY)],
            out_specs=out_specs,
        ),
        out_shape=out_shape,
        compiler_params=pltpu.CompilerParams(vmem_limit_bytes=VMEM_LIMIT),
        cost_estimate=pl.CostEstimate(flops=8 * rows * depth, bytes_accessed=20 * rows * depth, transcendentals=0),
    )(mine_pattern, other_pattern, mine, other, lists)
    return made if len(made) == 2 else (made[0], jnp.zeros((rows, blocks * TILE), jnp.float32))


def pack_kernel(lists_ref, *refs, plan, sources, at):
    ins, outs = refs[:sources], refs[sources:]
    for out, (base, size) in zip(outs, plan):

        def copy(slot, _, out=out, base=base):
            row = pl.multiple_of(lists_ref[at["row"] + base + slot], TILE)
            lane = pl.multiple_of(lists_ref[at["lane"] + base + slot], TILE)
            for source in range(sources):

                @pl.when(lists_ref[at["source"] + base + slot] == source)
                def _(source=source):
                    out[slot] = ins[source][pl.ds(row, TILE), pl.ds(lane, TILE)]

            return 0

        lax.fori_loop(0, size, copy, 0)


def pack(lists, at, sources, plan):
    whole = lambda x: pl.BlockSpec(x.shape, lambda g, *s: (0,) * len(x.shape))
    outs = [jax.ShapeDtypeStruct((size, TILE, TILE), jnp.float32) for _, size in plan]
    return pl.pallas_call(
        functools.partial(pack_kernel, plan=plan, sources=len(sources), at=at),
        grid_spec=pltpu.PrefetchScalarGridSpec(
            num_scalar_prefetch=1,
            grid=(1,),
            in_specs=[whole(x) for x in sources],
            out_specs=[whole(x) for x in outs],
        ),
        out_shape=outs,
        compiler_params=pltpu.CompilerParams(vmem_limit_bytes=VMEM_LIMIT),
        cost_estimate=pl.CostEstimate(
            flops=0, bytes_accessed=4 * (sum(x.size for x in sources) + sum(x.size for x in outs)), transcendentals=0
        ),
    )(lists, *sources)


def pool_kernel(lists_ref, *refs, at):
    *ins, out = refs
    for e, ref in enumerate(ins):

        def copy(slot, _, ref=ref, e=e):
            out[lists_ref[at["offsets"] + e] + slot] = ref[slot]
            return 0

        lax.fori_loop(0, lists_ref[at["sizes"] + e], copy, 0)


def pool(lists, at, arrays, capacity):
    whole = lambda shape: pl.BlockSpec(shape, lambda g, *s: (0,) * len(shape))
    shape = (capacity, TILE, TILE)
    return pl.pallas_call(
        functools.partial(pool_kernel, at=at),
        grid_spec=pltpu.PrefetchScalarGridSpec(
            num_scalar_prefetch=1,
            grid=(1,),
            in_specs=[whole(x.shape) for x in arrays],
            out_specs=whole(shape),
        ),
        out_shape=jax.ShapeDtypeStruct(shape, jnp.float32),
        compiler_params=pltpu.CompilerParams(vmem_limit_bytes=VMEM_LIMIT),
        cost_estimate=pl.CostEstimate(flops=0, bytes_accessed=12 * capacity * TILE * TILE, transcendentals=0),
    )(lists, *arrays)


def gate_kernel(*refs):
    del refs


def gate(released, awaited):
    anywhere = pl.BlockSpec(memory_space=pl.ANY)
    return pl.pallas_call(
        gate_kernel,
        in_specs=[anywhere] * (len(released) + len(awaited)),
        out_specs=[anywhere] * len(released),
        out_shape=[jax.ShapeDtypeStruct(x.shape, x.dtype) for x in released],
        input_output_aliases={i: i for i in range(len(released))},
    )(*released, *awaited)


def multiply_kernel(
    lists_ref, amp_ref, mine_in, other_in, *refs, at, turn, first, chips, segments, steps, per_chip, wide, long, straight
):
    def spot(g):
        column = g * wide
        e = column // per_chip
        return turn * chips + first + e, column - e * per_chip

    def low_of(g, i):
        listed, column = spot(g)
        return lists_ref[at["bounds"] + listed * (per_chip + 1) + column + i]

    count = len(segments)
    tiles = refs[:count]
    mine_ref, other_ref, buffer, sem = refs[count:]
    step = pl.program_id(0)
    rows = mine_ref.shape[0]

    def issue(g, half):
        low, high = low_of(g, 0), low_of(g, wide)
        for ref, (a, b, pooled, only) in zip(tiles, segments):
            shift = lists_ref[at["offsets"] + spot(g)[0]] - straight if pooled else -a

            def start(slot, _, ref=ref, shift=shift):
                pltpu.make_async_copy(
                    ref.at[slot + shift], buffer.at[half, slot - low], sem.at[half, slot - low]
                ).start()
                return 0

            first = jnp.maximum(low, a)
            last = jnp.maximum(first, jnp.minimum(high, b))
            if only is not None:
                last = jnp.where(g * wide // per_chip == only, last, first)
            lax.fori_loop(first, last, start, 0)

    half = lax.rem(step, 2)

    @pl.when(step == 0)
    def _():
        issue(0, 0)

    @pl.when(step + 1 < steps)
    def _():
        issue(step + 1, 1 - half)

    mine_ref[...] = mine_in[...]
    other_ref[...] = other_in[...]
    origin = low_of(step, 0)
    for i in range(wide):
        lanes = pl.ds(i * TILE, TILE)
        low = low_of(step, i)
        length = low_of(step, i + 1) - low
        base = at["kk"] + spot(step)[0] * long + low

        def wait(place, _, low=low):
            place = low - origin + place
            pltpu.make_async_copy(tiles[0].at[0], buffer.at[half, place], sem.at[half, place]).wait()
            return 0

        lax.fori_loop(0, length, wait, 0)

        def add(turn, _, lanes=lanes, low=low, length=length, base=base):
            weights, ks = [], []
            for u in range(UNROLL):
                place = turn * UNROLL + u
                inside = place < length
                place = jnp.minimum(place, length - 1)
                value = buffer[half, low - origin + place]
                if u:
                    value = jnp.where(inside, value, 0.0)
                high = value.astype(jnp.bfloat16)
                rest = (value - high.astype(jnp.float32)).astype(jnp.bfloat16)
                weights.append(jnp.concatenate([high, rest], axis=1))
                weights.append(jnp.concatenate([high, jnp.zeros_like(high)], axis=1))
                ks.append(lists_ref[base + place])
            left = jnp.concatenate([amp_ref[k] for k in ks], axis=1)
            product = jnp.dot(left, jnp.concatenate(weights, axis=0), preferred_element_type=jnp.float32)
            total = product[:, :TILE] + product[:, TILE:]
            mine_ref[:, lanes] += total[:rows]
            other_ref[:, lanes] += total[rows:]
            return 0

        lax.fori_loop(0, (length + UNROLL - 1) // UNROLL, add, 0)


def multiply(lists, at, turn, first, count, chips, per_chip, wide, long, straight, amps, mine, other, pieces, kd, spot):
    rows = mine.shape[0]
    segments = [piece[1:] for piece in pieces]
    blocks = per_chip // wide
    steps = count * blocks
    expected = 10 * steps * wide
    n = 1
    mine_spec = pl.BlockSpec((rows, wide * TILE), lambda g, s: (0, s[at["mine"] + first * blocks + g]))
    other_spec = pl.BlockSpec((rows, wide * TILE), lambda g, s: (0, spot * blocks + g))
    anywhere = pl.BlockSpec(memory_space=pl.ANY)
    held = CORES * kd * wide
    return pl.pallas_call(
        functools.partial(
            multiply_kernel,
            at=at,
            turn=turn,
            first=first,
            chips=chips,
            segments=segments,
            steps=steps,
            per_chip=per_chip,
            wide=wide,
            long=long,
            straight=straight,
        ),
        grid_spec=pltpu.PrefetchScalarGridSpec(
            num_scalar_prefetch=n,
            grid=(steps,),
            in_specs=[
                pl.BlockSpec((CORES * kd, CORES * rows, 2 * TILE), lambda g, s: (s[at["planes"] + turn], 0, 0)),
                mine_spec,
                other_spec,
            ]
            + [anywhere] * len(pieces),
            out_specs=[mine_spec, other_spec],
            scratch_shapes=[pltpu.VMEM((2, held, TILE, TILE), jnp.float32), pltpu.SemaphoreType.DMA((2, held))],
        ),
        out_shape=[jax.ShapeDtypeStruct(x.shape, x.dtype) for x in (mine, other)],
        input_output_aliases={n + 1: 0, n + 2: 1},
        compiler_params=pltpu.CompilerParams(vmem_limit_bytes=VMEM_LIMIT),
        cost_estimate=pl.CostEstimate(
            flops=expected * 32 * rows * TILE * TILE,
            bytes_accessed=expected * 4 * TILE * TILE,
            transcendentals=0,
        ),
    )(lists, amps, mine, other, *[piece[0] for piece in pieces])


def place_kernel(at_ref, mine_in, piece_ref, out_ref):
    out_ref[...] = mine_in[...] + piece_ref[...]


def place(at, wide, mine, piece):
    rows = mine.shape[0]
    spec = pl.BlockSpec((rows, wide * TILE), lambda g, a: (0, a[g]))
    return pl.pallas_call(
        place_kernel,
        grid_spec=pltpu.PrefetchScalarGridSpec(
            num_scalar_prefetch=1,
            grid=(at.shape[0],),
            in_specs=[spec, pl.BlockSpec((rows, wide * TILE), lambda g, a: (0, g))],
            out_specs=spec,
        ),
        out_shape=jax.ShapeDtypeStruct(mine.shape, mine.dtype),
        input_output_aliases={1: 0},
        compiler_params=pltpu.CompilerParams(vmem_limit_bytes=VMEM_LIMIT),
        cost_estimate=pl.CostEstimate(flops=piece.size, bytes_accessed=12 * piece.size, transcendentals=0),
    )(at, mine, piece)


def body(amplitudes, integrals, amp_pattern, int_pattern, *, chips, devices):
    R, Z = chips, devices // CORES
    first, second, depth = amplitudes.shape
    rows = first * second
    kd = integrals.shape[0] // TILE
    ntl = integrals.shape[1] // TILE
    groups = R if ntl % R == 0 else 1
    width = ntl // groups
    if groups == 4:
        wide = width
        owned = [[d * width + i for d in pair for i in range(width)] for pair in ((0, 3), (1, 2))]
    else:
        wide = 1
        owned = [list(range(c, ntl, CORES)) for c in range(CORES)]
        owned = [x + [ntl] * (len(owned[0]) - len(x)) for x in owned]
    per_chip = len(owned[0])
    tiles = per_chip * CORES * kd

    r = lax.axis_index("row")
    col = lax.axis_index("col")
    core = lax.rem(col, CORES)
    ring = [0] + list(range(1, Z, 2)) + [z for z in range(Z - 1, 0, -1) if z % 2 == 0]
    spot = [ring.index(z) for z in range(Z)]

    def by_row(x, distance):
        return lax.ppermute(x, "row", [(a, a ^ distance) for a in range(R)])

    def by_core(x):
        return lax.ppermute(x, "col", [(a, a ^ 1) for a in range(Z * CORES)])

    def by_plane(x):
        return lax.ppermute(
            x,
            "col",
            [(ring[a] * CORES + c, ring[(a + 1) % Z] * CORES + c) for a in range(Z) for c in range(CORES)],
        )

    blocks = R * ntl
    spare = per_chip * CORES - ntl
    parts_of = [[0], [1, 2], [3]] if R == 4 else [list(range(R))]
    others = [jnp.zeros((rows, len(part) * per_chip * TILE), jnp.float32) for part in parts_of]
    shares = [integrals[:, d * width * TILE : (d + 1) * width * TILE] for d in range(groups)]
    if groups > 1:
        (int_pattern,) = gate([int_pattern], shares[1:])
    for d in range(1, groups):
        shares[d] = by_row(shares[d], d)

    patterns = [int_pattern] + [by_row(int_pattern, d) for d in range(1, R)]
    by_distance = jnp.stack(patterns).reshape(R, Z, CORES * kd, groups, width)
    near = []
    for e in range(R):
        picked = jnp.stack([by_distance[e ^ d, :, :, d] for d in range(groups)], axis=2)
        near.append(picked.reshape(Z, CORES * kd, ntl))
    present = (jnp.stack(near, axis=1) != 0).astype(jnp.int32)
    present = jnp.pad(present, ((0, 0), (0, 0), (0, 0), (0, per_chip * CORES - ntl)))
    present = jnp.stack([jnp.stack([present[..., j] for j in x], axis=-1) for x in owned], axis=-1)
    present = present.transpose(0, 1, 4, 3, 2)
    both = present.reshape(Z, R, CORES, tiles)
    cores_counts = jnp.sum(both, axis=-1)
    own = jnp.where(core == 0, both[:, :, 0], both[:, :, 1])
    here = jnp.asarray(spot)[col // CORES]
    planes = jnp.asarray(ring)[lax.rem(here - jnp.arange(Z) + Z, Z)]
    if R == 4:
        own = jnp.stack(
            [
                own[:, 0],
                jnp.where(core == 0, own[:, 1], own[:, 2]),
                jnp.where(core == 0, own[:, 2], own[:, 1]),
                own[:, 3],
            ],
            axis=1,
        )
    own = own[planes]
    counts = jnp.sum(own, axis=-1)
    ids = jnp.arange(tiles)
    slot_of = jnp.sum(own[..., None, :] * (ids[None, :] < ids[:, None]), axis=-1)
    slots = (
        jnp.sum(
            (ids + 1)[None, None, None, :]
            * ((slot_of[:, :, None, :] == ids[:, None]) & (own[:, :, None, :] > 0)),
            axis=-1,
        )
        - 1
    )
    ends = jnp.sum(own[:, :, None, :] * (ids[None, :] < (jnp.arange(per_chip + 1) * CORES * kd)[:, None]), axis=-1)

    straight = max(2, round(tiles * 38 / 72)) if R == 4 else max(4, 2 * round(tiles * 25 / 72))
    extra = max(2, round(tiles * 12 / 72)) if R == 4 else 0
    pooled = max(R, round(tiles * 20 / 72)) if R == 4 else 0
    longest = tiles + straight + extra
    slots = jnp.pad(slots, ((0, 0), (0, 0), (0, longest - tiles)), constant_values=-1)
    most = jnp.max(cores_counts)

    def chips_of(which):
        return r ^ (jnp.stack([0 * which, 1 + which, 2 - which, 0 * which + 3]) if R == 4 else jnp.arange(R))

    chip_of = chips_of(core)

    def columns_of(which):
        column = jnp.asarray(owned)[which][None, ::wide]
        group = column // width
        chip = chips_of(which)[:, None]
        at = (((chip ^ group) if groups > 1 else chip) * groups + group) * width + column % width
        return (jnp.where(column < ntl, at, blocks) // wide).astype(jnp.int32)

    mine_at = columns_of(core)
    received_at = columns_of(1 - core)

    def across(x, near):
        return lax.ppermute(
            x,
            ("row", "col"),
            [
                (a * devices + d, (a ^ (near if d % CORES == 0 else 3 - near)) * devices + d)
                for a in range(R)
                for d in range(devices)
            ],
        )

    def listed(base):
        after = base + straight
        left = jnp.clip(cores_counts - after, 0, extra)
        fits = jnp.max(jnp.sum(left, axis=1)) <= pooled
        taken = jnp.where(fits, extra, pooled // R) if extra else jnp.int32(0)
        sizes = jnp.clip(counts - after, 0, taken)
        before = chip_of[None, :] < chip_of[:, None]
        offsets = jnp.sum(sizes[:, None, :] * before[None], axis=-1)
        now = lax.dynamic_slice_in_dim(slots, base, straight + extra, axis=2)
        kk = jnp.maximum(now, 0) % (CORES * kd)
        bounds = jnp.clip(ends - base, 0, straight + taken)
        column = jnp.asarray(owned)[core][jnp.maximum(now[0, 0], 0) // (CORES * kd)]
        holder = kk[0, 0] // kd
        source = jnp.where(now[0, 0] < 0, -1, (holder != core) * groups + column // width)
        found = {
            "source": source,
            "row": kk[0, 0] % kd * TILE,
            "lane": column % width * TILE,
            "sizes": sizes,
            "offsets": offsets,
            "bounds": bounds,
            "kk": kk,
            "mine": mine_at,
            "planes": planes,
        }
        at, total = {}, 0
        for name, x in found.items():
            at[name] = total
            total += x.size
        return jnp.concatenate([x.reshape(-1).astype(jnp.int32) for x in found.values()]), at, taken

    first_lists = listed(jnp.int32(0))
    amps_mine = amplitudes.reshape(rows, depth)
    amps, mine = split_amplitudes(
        amps_mine, by_core(amps_mine), amp_pattern, by_core(amp_pattern), first_lists[0], second, blocks + spare
    )
    if groups > 1:
        shares[1:] = gate(shares[1:], [amps])
    twins = [by_core(x) for x in shares]

    def one_round(state, others, made):
        base, mine = state
        others = list(others)
        lists, at, taken = made
        plan = ((0, straight), (straight, extra), (0, straight)) if extra else ((0, straight),)
        packed = pack(lists, at, shares + twins, plan)

        def add(mine, other, step, neighbours, pieces, spot=0):
            return multiply(
                lists,
                at,
                step,
                neighbours[0],
                len(neighbours),
                R,
                per_chip,
                wide,
                straight + extra,
                straight,
                amps,
                mine,
                other,
                pieces,
                kd,
                spot,
            )

        if R == 4:
            end = straight + extra
            sent, late, ready = packed
            along = [sent, by_plane(sent)]
            first_late, second_late = across(late, 1), across(late, 2)
            at_home = [(sent, 0, straight, False, None), (late, straight, end, False, None)]
            mine, others[0] = add(mine, others[0], 0, [0], at_home)
            first_late, ready, mine = gate([first_late, ready, mine], [second_late])
            third_late = across(first_late, 2)
            first_near, second_near = across(ready, 1), across(ready, 2)
            pools = [
                pool(
                    lists,
                    at,
                    [late, first_late, second_late, third_late],
                    pooled,
                )
            ]
            pools.append(by_plane(pools[0]))
            received = []
            for step in range(Z):
                first_near, mine = gate([first_near, mine], [second_near, pools[step]])
                third_near = across(first_near, 2)
                mixed = (pools[step], straight, end, True, None)
                near = [(first_near, 0, straight, False, 0), (second_near, 0, straight, False, 1), mixed]
                last = [(third_near, 0, straight, False, None), mixed]
                if step:
                    home = [(along[step], 0, straight, False, None), mixed]
                    mine, others[0] = add(mine, others[0], step, [0], home)
                if step == Z - 1:
                    received.append(by_core(others[0]))
                else:
                    along[step + 1], mine = gate([along[step + 1], mine], [third_near])
                    first_near, second_near = across(along[step + 1], 1), across(along[step + 1], 2)
                    if step + 2 < Z:
                        along.append(by_plane(along[step + 1]))
                        pools.append(by_plane(pools[step + 1]))
                mine, others[1] = add(mine, others[1], step, [1, 2], near)
                if step == Z - 1:
                    received.append(by_core(others[1]))
                    mine = place(received_at[0], wide, mine, received[0])
                mine, others[2] = add(mine, others[2], step, [3], last)
            received.append(by_core(others[2]))
            mine = place(received_at[1:3].reshape(-1), wide, mine, received[1])
            mine = place(received_at[3], wide, mine, received[2])
        else:
            now_at = packed[0]
            for step in range(Z):
                for e in range(R):
                    piece = by_row(now_at, e) if e else now_at
                    mine, others[0] = add(mine, others[0], step, [e], [(piece, 0, straight, False, None)], e)
                if step + 1 < Z:
                    now_at = by_plane(now_at)
            mine = place(received_at.reshape(-1), wide, mine, by_core(others[0]))
        return base + straight + taken, mine

    state = one_round((jnp.int32(0), mine), others, first_lists)
    cleared = [x.shape for x in others]
    _, mine = lax.while_loop(
        lambda state: state[0] < most,
        lambda state: one_round(state, [jnp.zeros(shape, jnp.float32) for shape in cleared], listed(state[0])),
        state,
    )
    return mine[:, : blocks * TILE].reshape(first, second, blocks * TILE)


def solution(mesh):
    placed = (P("col", "row", None), P("col", "row"), P("col", None), P(None, "row"))
    return jax.shard_map(
        functools.partial(body, chips=mesh.shape["row"], devices=mesh.shape["col"]),
        mesh=mesh,
        in_specs=placed,
        out_specs=P("col", "row", None),
        check_vma=False,
    )
```

```python
import functools

import jax
import jax.numpy as jnp
from jax import lax
from jax.experimental import pallas as pl
from jax.experimental.pallas import tpu as pltpu
from jax.sharding import PartitionSpec as P

TILE = 128
CORES = 2
UNROLL = 3
VMEM_LIMIT = 48 * 1024 * 1024


def split_kernel(mine_pattern, other_pattern, mine_ref, other_ref, lists_ref, out_ref, *cleared, second, deep):
    del lists_ref
    rows = mine_ref.shape[0]
    for ref in cleared:
        ref[...] = jnp.zeros_like(ref)
    for i in range(deep):
        k = pl.program_id(0) * deep + i
        lanes = pl.ds(i * TILE, TILE)
        for half, (pattern, amp_ref) in enumerate(((mine_pattern, mine_ref), (other_pattern, other_ref))):
            for first in range(rows // second):
                value = amp_ref[pl.ds(first * second, second), lanes] * pattern[first, k].astype(jnp.float32)
                high = value.astype(jnp.bfloat16)
                low = (value - high.astype(jnp.float32)).astype(jnp.bfloat16)
                here = pl.ds(half * rows + first * second, second)
                out_ref[i, here, :TILE] = high
                out_ref[i, here, TILE:] = low


def split_amplitudes(mine, other, mine_pattern, other_pattern, lists, second, blocks):
    rows, depth = mine.shape
    tiles = depth // TILE
    deep = 4 if tiles % 4 == 0 else 1
    steps = tiles // deep
    out_shape = [jax.ShapeDtypeStruct((tiles, CORES * rows, 2 * TILE), jnp.bfloat16)]
    out_specs = [pl.BlockSpec((deep, CORES * rows, 2 * TILE), lambda k, *_: (k, 0, 0))]
    if blocks % steps == 0:
        out_shape.append(jax.ShapeDtypeStruct((rows, blocks * TILE), jnp.float32))
        out_specs.append(pl.BlockSpec((rows, blocks // steps * TILE), lambda k, *_: (0, k)))
    made = pl.pallas_call(
        functools.partial(split_kernel, second=second, deep=deep),
        grid_spec=pltpu.PrefetchScalarGridSpec(
            num_scalar_prefetch=2,
            grid=(steps,),
            in_specs=[pl.BlockSpec((rows, deep * TILE), lambda k, *_: (0, k))] * 2 + [pl.BlockSpec(memory_space=pl.ANY)],
            out_specs=out_specs,
        ),
        out_shape=out_shape,
        compiler_params=pltpu.CompilerParams(vmem_limit_bytes=VMEM_LIMIT),
        cost_estimate=pl.CostEstimate(flops=8 * rows * depth, bytes_accessed=20 * rows * depth, transcendentals=0),
    )(mine_pattern, other_pattern, mine, other, lists)
    return made if len(made) == 2 else (made[0], jnp.zeros((rows, blocks * TILE), jnp.float32))


def pack_kernel(lists_ref, *refs, plan, sources, at):
    ins, outs = refs[:sources], refs[sources:]
    for out, (base, size) in zip(outs, plan):

        def copy(slot, _, out=out, base=base):
            row = pl.multiple_of(lists_ref[at["row"] + base + slot], TILE)
            lane = pl.multiple_of(lists_ref[at["lane"] + base + slot], TILE)
            for source in range(sources):

                @pl.when(lists_ref[at["source"] + base + slot] == source)
                def _(source=source):
                    out[slot] = ins[source][pl.ds(row, TILE), pl.ds(lane, TILE)]

            return 0

        lax.fori_loop(0, size, copy, 0)


def pack(lists, at, sources, plan):
    whole = lambda x: pl.BlockSpec(x.shape, lambda g, *s: (0,) * len(x.shape))
    outs = [jax.ShapeDtypeStruct((size, TILE, TILE), jnp.float32) for _, size in plan]
    return pl.pallas_call(
        functools.partial(pack_kernel, plan=plan, sources=len(sources), at=at),
        grid_spec=pltpu.PrefetchScalarGridSpec(
            num_scalar_prefetch=1,
            grid=(1,),
            in_specs=[whole(x) for x in sources],
            out_specs=[whole(x) for x in outs],
        ),
        out_shape=outs,
        compiler_params=pltpu.CompilerParams(vmem_limit_bytes=VMEM_LIMIT),
        cost_estimate=pl.CostEstimate(
            flops=0, bytes_accessed=4 * (sum(x.size for x in sources) + sum(x.size for x in outs)), transcendentals=0
        ),
    )(lists, *sources)


def pool_kernel(lists_ref, *refs, at):
    *ins, out = refs
    for e, ref in enumerate(ins):

        def copy(slot, _, ref=ref, e=e):
            out[lists_ref[at["offsets"] + e] + slot] = ref[slot]
            return 0

        lax.fori_loop(0, lists_ref[at["sizes"] + e], copy, 0)


def pool(lists, at, arrays, capacity):
    whole = lambda shape: pl.BlockSpec(shape, lambda g, *s: (0,) * len(shape))
    shape = (capacity, TILE, TILE)
    return pl.pallas_call(
        functools.partial(pool_kernel, at=at),
        grid_spec=pltpu.PrefetchScalarGridSpec(
            num_scalar_prefetch=1,
            grid=(1,),
            in_specs=[whole(x.shape) for x in arrays],
            out_specs=whole(shape),
        ),
        out_shape=jax.ShapeDtypeStruct(shape, jnp.float32),
        compiler_params=pltpu.CompilerParams(vmem_limit_bytes=VMEM_LIMIT),
        cost_estimate=pl.CostEstimate(flops=0, bytes_accessed=12 * capacity * TILE * TILE, transcendentals=0),
    )(lists, *arrays)


def gate_kernel(*refs):
    del refs


def gate(released, awaited):
    anywhere = pl.BlockSpec(memory_space=pl.ANY)
    return pl.pallas_call(
        gate_kernel,
        in_specs=[anywhere] * (len(released) + len(awaited)),
        out_specs=[anywhere] * len(released),
        out_shape=[jax.ShapeDtypeStruct(x.shape, x.dtype) for x in released],
        input_output_aliases={i: i for i in range(len(released))},
    )(*released, *awaited)


def multiply_kernel(
    lists_ref, amp_ref, mine_in, other_in, *refs, at, turn, first, chips, segments, steps, per_chip, wide, long, straight
):
    def spot(g):
        column = g * wide
        e = column // per_chip
        return turn * chips + first + e, column - e * per_chip

    def low_of(g, i):
        listed, column = spot(g)
        return lists_ref[at["bounds"] + listed * (per_chip + 1) + column + i]

    count = len(segments)
    tiles = refs[:count]
    mine_ref, other_ref, buffer, sem = refs[count:]
    step = pl.program_id(0)
    rows = mine_ref.shape[0]

    def issue(g, half):
        low, high = low_of(g, 0), low_of(g, wide)
        for ref, (a, b, pooled, only) in zip(tiles, segments):
            shift = lists_ref[at["offsets"] + spot(g)[0]] - straight if pooled else -a

            def start(slot, _, ref=ref, shift=shift):
                pltpu.make_async_copy(
                    ref.at[slot + shift], buffer.at[half, slot - low], sem.at[half, slot - low]
                ).start()
                return 0

            first = jnp.maximum(low, a)
            last = jnp.maximum(first, jnp.minimum(high, b))
            if only is not None:
                last = jnp.where(g * wide // per_chip == only, last, first)
            lax.fori_loop(first, last, start, 0)

    half = lax.rem(step, 2)

    @pl.when(step == 0)
    def _():
        issue(0, 0)

    @pl.when(step + 1 < steps)
    def _():
        issue(step + 1, 1 - half)

    mine_ref[...] = mine_in[...]
    other_ref[...] = other_in[...]
    origin = low_of(step, 0)
    for i in range(wide):
        lanes = pl.ds(i * TILE, TILE)
        low = low_of(step, i)
        length = low_of(step, i + 1) - low
        base = at["kk"] + spot(step)[0] * long + low

        def wait(place, _, low=low):
            place = low - origin + place
            pltpu.make_async_copy(tiles[0].at[0], buffer.at[half, place], sem.at[half, place]).wait()
            return 0

        lax.fori_loop(0, length, wait, 0)

        def add(turn, _, lanes=lanes, low=low, length=length, base=base):
            weights, ks = [], []
            for u in range(UNROLL):
                place = turn * UNROLL + u
                inside = place < length
                place = jnp.minimum(place, length - 1)
                value = buffer[half, low - origin + place]
                if u:
                    value = jnp.where(inside, value, 0.0)
                high = value.astype(jnp.bfloat16)
                rest = (value - high.astype(jnp.float32)).astype(jnp.bfloat16)
                weights.append(jnp.concatenate([high, rest], axis=1))
                weights.append(jnp.concatenate([high, jnp.zeros_like(high)], axis=1))
                ks.append(lists_ref[base + place])
            left = jnp.concatenate([amp_ref[k] for k in ks], axis=1)
            product = jnp.dot(left, jnp.concatenate(weights, axis=0), preferred_element_type=jnp.float32)
            total = product[:, :TILE] + product[:, TILE:]
            mine_ref[:, lanes] += total[:rows]
            other_ref[:, lanes] += total[rows:]
            return 0

        lax.fori_loop(0, (length + UNROLL - 1) // UNROLL, add, 0)


def multiply(lists, at, turn, first, count, chips, per_chip, wide, long, straight, amps, mine, other, pieces, kd, spot):
    rows = mine.shape[0]
    segments = [piece[1:] for piece in pieces]
    blocks = per_chip // wide
    steps = count * blocks
    expected = 10 * steps * wide
    n = 1
    mine_spec = pl.BlockSpec((rows, wide * TILE), lambda g, s: (0, s[at["mine"] + first * blocks + g]))
    other_spec = pl.BlockSpec((rows, wide * TILE), lambda g, s: (0, spot * blocks + g))
    anywhere = pl.BlockSpec(memory_space=pl.ANY)
    held = CORES * kd * wide
    return pl.pallas_call(
        functools.partial(
            multiply_kernel,
            at=at,
            turn=turn,
            first=first,
            chips=chips,
            segments=segments,
            steps=steps,
            per_chip=per_chip,
            wide=wide,
            long=long,
            straight=straight,
        ),
        grid_spec=pltpu.PrefetchScalarGridSpec(
            num_scalar_prefetch=n,
            grid=(steps,),
            in_specs=[
                pl.BlockSpec((CORES * kd, CORES * rows, 2 * TILE), lambda g, s: (s[at["planes"] + turn], 0, 0)),
                mine_spec,
                other_spec,
            ]
            + [anywhere] * len(pieces),
            out_specs=[mine_spec, other_spec],
            scratch_shapes=[pltpu.VMEM((2, held, TILE, TILE), jnp.float32), pltpu.SemaphoreType.DMA((2, held))],
        ),
        out_shape=[jax.ShapeDtypeStruct(x.shape, x.dtype) for x in (mine, other)],
        input_output_aliases={n + 1: 0, n + 2: 1},
        compiler_params=pltpu.CompilerParams(vmem_limit_bytes=VMEM_LIMIT),
        cost_estimate=pl.CostEstimate(
            flops=expected * 32 * rows * TILE * TILE,
            bytes_accessed=expected * 4 * TILE * TILE,
            transcendentals=0,
        ),
    )(lists, amps, mine, other, *[piece[0] for piece in pieces])


def place_kernel(at_ref, mine_in, piece_ref, out_ref):
    out_ref[...] = mine_in[...] + piece_ref[...]


def place(at, wide, mine, piece):
    rows = mine.shape[0]
    spec = pl.BlockSpec((rows, wide * TILE), lambda g, a: (0, a[g]))
    return pl.pallas_call(
        place_kernel,
        grid_spec=pltpu.PrefetchScalarGridSpec(
            num_scalar_prefetch=1,
            grid=(at.shape[0],),
            in_specs=[spec, pl.BlockSpec((rows, wide * TILE), lambda g, a: (0, g))],
            out_specs=spec,
        ),
        out_shape=jax.ShapeDtypeStruct(mine.shape, mine.dtype),
        input_output_aliases={1: 0},
        compiler_params=pltpu.CompilerParams(vmem_limit_bytes=VMEM_LIMIT),
        cost_estimate=pl.CostEstimate(flops=piece.size, bytes_accessed=12 * piece.size, transcendentals=0),
    )(at, mine, piece)


def body(amplitudes, integrals, amp_pattern, int_pattern, *, chips, devices):
    R, Z = chips, devices // CORES
    first, second, depth = amplitudes.shape
    rows = first * second
    kd = integrals.shape[0] // TILE
    ntl = integrals.shape[1] // TILE
    groups = R if ntl % R == 0 else 1
    width = ntl // groups
    if groups == 4:
        wide = width
        owned = [[d * width + i for d in pair for i in range(width)] for pair in ((0, 3), (1, 2))]
    else:
        wide = 1
        owned = [list(range(c, ntl, CORES)) for c in range(CORES)]
        owned = [x + [ntl] * (len(owned[0]) - len(x)) for x in owned]
    per_chip = len(owned[0])
    tiles = per_chip * CORES * kd

    r = lax.axis_index("row")
    col = lax.axis_index("col")
    core = lax.rem(col, CORES)
    ring = [0] + list(range(1, Z, 2)) + [z for z in range(Z - 1, 0, -1) if z % 2 == 0]
    spot = [ring.index(z) for z in range(Z)]

    def by_row(x, distance):
        return lax.ppermute(x, "row", [(a, a ^ distance) for a in range(R)])

    def by_core(x):
        return lax.ppermute(x, "col", [(a, a ^ 1) for a in range(Z * CORES)])

    def by_plane(x):
        return lax.ppermute(
            x,
            "col",
            [(ring[a] * CORES + c, ring[(a + 1) % Z] * CORES + c) for a in range(Z) for c in range(CORES)],
        )

    blocks = R * ntl
    spare = per_chip * CORES - ntl
    parts_of = [[0], [1, 2], [3]] if R == 4 else [list(range(R))]
    others = [jnp.zeros((rows, len(part) * per_chip * TILE), jnp.float32) for part in parts_of]
    shares = [integrals[:, d * width * TILE : (d + 1) * width * TILE] for d in range(groups)]
    if groups > 1:
        (int_pattern,) = gate([int_pattern], shares[1:])
    for d in range(1, groups):
        shares[d] = by_row(shares[d], d)

    patterns = [int_pattern] + [by_row(int_pattern, d) for d in range(1, R)]
    by_distance = jnp.stack(patterns).reshape(R, Z, CORES * kd, groups, width)
    near = []
    for e in range(R):
        picked = jnp.stack([by_distance[e ^ d, :, :, d] for d in range(groups)], axis=2)
        near.append(picked.reshape(Z, CORES * kd, ntl))
    present = (jnp.stack(near, axis=1) != 0).astype(jnp.int32)
    present = jnp.pad(present, ((0, 0), (0, 0), (0, 0), (0, per_chip * CORES - ntl)))
    present = jnp.stack([jnp.stack([present[..., j] for j in x], axis=-1) for x in owned], axis=-1)
    present = present.transpose(0, 1, 4, 3, 2)
    both = present.reshape(Z, R, CORES, tiles)
    cores_counts = jnp.sum(both, axis=-1)
    own = jnp.where(core == 0, both[:, :, 0], both[:, :, 1])
    here = jnp.asarray(spot)[col // CORES]
    planes = jnp.asarray(ring)[lax.rem(here - jnp.arange(Z) + Z, Z)]
    if R == 4:
        own = jnp.stack(
            [
                own[:, 0],
                jnp.where(core == 0, own[:, 1], own[:, 2]),
                jnp.where(core == 0, own[:, 2], own[:, 1]),
                own[:, 3],
            ],
            axis=1,
        )
    own = own[planes]
    counts = jnp.sum(own, axis=-1)
    ids = jnp.arange(tiles)
    slot_of = jnp.sum(own[..., None, :] * (ids[None, :] < ids[:, None]), axis=-1)
    slots = (
        jnp.sum(
            (ids + 1)[None, None, None, :]
            * ((slot_of[:, :, None, :] == ids[:, None]) & (own[:, :, None, :] > 0)),
            axis=-1,
        )
        - 1
    )
    ends = jnp.sum(own[:, :, None, :] * (ids[None, :] < (jnp.arange(per_chip + 1) * CORES * kd)[:, None]), axis=-1)

    straight = max(2, round(tiles * 37 / 72)) if R == 4 else max(4, 2 * round(tiles * 25 / 72))
    extra = max(2, round(tiles * 13 / 72)) if R == 4 else 0
    pooled = max(R, round(tiles * 23 / 72)) if R == 4 else 0
    longest = tiles + straight + extra
    slots = jnp.pad(slots, ((0, 0), (0, 0), (0, longest - tiles)), constant_values=-1)
    most = jnp.max(cores_counts)

    def chips_of(which):
        return r ^ (jnp.stack([0 * which, 1 + which, 2 - which, 0 * which + 3]) if R == 4 else jnp.arange(R))

    chip_of = chips_of(core)

    def columns_of(which):
        column = jnp.asarray(owned)[which][None, ::wide]
        group = column // width
        chip = chips_of(which)[:, None]
        at = (((chip ^ group) if groups > 1 else chip) * groups + group) * width + column % width
        return (jnp.where(column < ntl, at, blocks) // wide).astype(jnp.int32)

    mine_at = columns_of(core)
    received_at = columns_of(1 - core)

    def across(x, near):
        return lax.ppermute(
            x,
            ("row", "col"),
            [
                (a * devices + d, (a ^ (near if d % CORES == 0 else 3 - near)) * devices + d)
                for a in range(R)
                for d in range(devices)
            ],
        )

    def listed(base):
        after = base + straight
        left = jnp.clip(cores_counts - after, 0, extra)
        fits = jnp.max(jnp.sum(left, axis=1)) <= pooled
        taken = jnp.where(fits, extra, pooled // R) if extra else jnp.int32(0)
        sizes = jnp.clip(counts - after, 0, taken)
        before = chip_of[None, :] < chip_of[:, None]
        offsets = jnp.sum(sizes[:, None, :] * before[None], axis=-1)
        now = lax.dynamic_slice_in_dim(slots, base, straight + extra, axis=2)
        kk = jnp.maximum(now, 0) % (CORES * kd)
        bounds = jnp.clip(ends - base, 0, straight + taken)
        column = jnp.asarray(owned)[core][jnp.maximum(now[0, 0], 0) // (CORES * kd)]
        holder = kk[0, 0] // kd
        source = jnp.where(now[0, 0] < 0, -1, (holder != core) * groups + column // width)
        found = {
            "source": source,
            "row": kk[0, 0] % kd * TILE,
            "lane": column % width * TILE,
            "sizes": sizes,
            "offsets": offsets,
            "bounds": bounds,
            "kk": kk,
            "mine": mine_at,
            "planes": planes,
        }
        at, total = {}, 0
        for name, x in found.items():
            at[name] = total
            total += x.size
        return jnp.concatenate([x.reshape(-1).astype(jnp.int32) for x in found.values()]), at, taken

    first_lists = listed(jnp.int32(0))
    amps_mine = amplitudes.reshape(rows, depth)
    amps, mine = split_amplitudes(
        amps_mine, by_core(amps_mine), amp_pattern, by_core(amp_pattern), first_lists[0], second, blocks + spare
    )
    if groups > 1:
        shares[1:] = gate(shares[1:], [amps])
    twins = [by_core(x) for x in shares]

    def one_round(state, others, made):
        base, mine = state
        others = list(others)
        lists, at, taken = made
        plan = ((0, straight), (straight, extra), (0, straight)) if extra else ((0, straight),)
        packed = pack(lists, at, shares + twins, plan)

        def add(mine, other, step, neighbours, pieces, spot=0):
            return multiply(
                lists,
                at,
                step,
                neighbours[0],
                len(neighbours),
                R,
                per_chip,
                wide,
                straight + extra,
                straight,
                amps,
                mine,
                other,
                pieces,
                kd,
                spot,
            )

        if R == 4:
            end = straight + extra
            sent, late, ready = packed
            along = [sent, by_plane(sent)]
            first_late, second_late = across(late, 1), across(late, 2)
            at_home = [(sent, 0, straight, False, None), (late, straight, end, False, None)]
            mine, others[0] = add(mine, others[0], 0, [0], at_home)
            first_late, ready, mine = gate([first_late, ready, mine], [second_late])
            third_late = across(first_late, 2)
            first_near, second_near = across(ready, 1), across(ready, 2)
            pools = [
                pool(
                    lists,
                    at,
                    [late, first_late, second_late, third_late],
                    pooled,
                )
            ]
            pools.append(by_plane(pools[0]))
            received = []
            for step in range(Z):
                mixed = (pools[step], straight, end, True, None)
                if step:
                    home = [(along[step], 0, straight, False, None), mixed]
                    mine, others[0] = add(mine, others[0], step, [0], home)
                if step == Z - 1:
                    received.append(by_core(others[0]))
                first_near, mine = gate([first_near, mine], [second_near, pools[step], along[step if step else 1]])
                third_near = across(first_near, 2)
                near = [(first_near, 0, straight, False, 0), (second_near, 0, straight, False, 1), mixed]
                last = [(third_near, 0, straight, False, None), mixed]
                mine, others[1] = add(mine, others[1], step, [1, 2], near)
                if step == Z - 1:
                    received.append(by_core(others[1]))
                    mine = place(received_at[0], wide, mine, received[0])
                else:
                    along[step + 1], pools[step + 1], mine = gate(
                        [along[step + 1], pools[step + 1], mine], [third_near]
                    )
                    first_near, second_near = across(along[step + 1], 1), across(along[step + 1], 2)
                    if step + 2 < Z:
                        along.append(by_plane(along[step + 1]))
                        pools.append(by_plane(pools[step + 1]))
                mine, others[2] = add(mine, others[2], step, [3], last)
            received.append(by_core(others[2]))
            mine = place(received_at[1:3].reshape(-1), wide, mine, received[1])
            mine = place(received_at[3], wide, mine, received[2])
        else:
            now_at = packed[0]
            for step in range(Z):
                for e in range(R):
                    piece = by_row(now_at, e) if e else now_at
                    mine, others[0] = add(mine, others[0], step, [e], [(piece, 0, straight, False, None)], e)
                if step + 1 < Z:
                    now_at = by_plane(now_at)
            mine = place(received_at.reshape(-1), wide, mine, by_core(others[0]))
        return base + straight + taken, mine

    state = one_round((jnp.int32(0), mine), others, first_lists)
    cleared = [x.shape for x in others]
    _, mine = lax.while_loop(
        lambda state: state[0] < most,
        lambda state: one_round(state, [jnp.zeros(shape, jnp.float32) for shape in cleared], listed(state[0])),
        state,
    )
    return mine[:, : blocks * TILE].reshape(first, second, blocks * TILE)


def solution(mesh):
    placed = (P("col", "row", None), P("col", "row"), P("col", None), P(None, "row"))
    return jax.shard_map(
        functools.partial(body, chips=mesh.shape["row"], devices=mesh.shape["col"]),
        mesh=mesh,
        in_specs=placed,
        out_specs=P("col", "row", None),
        check_vma=False,
    )
```

```python
import functools

import jax
import jax.numpy as jnp
from jax import lax
from jax.experimental import pallas as pl
from jax.experimental.pallas import tpu as pltpu
from jax.sharding import PartitionSpec as P

TILE = 128
CORES = 2
UNROLL = 3
VMEM_LIMIT = 48 * 1024 * 1024


def split_kernel(mine_pattern, other_pattern, mine_ref, other_ref, lists_ref, out_ref, *cleared, second, deep):
    del lists_ref
    rows = mine_ref.shape[0]
    for ref in cleared:
        ref[...] = jnp.zeros_like(ref)
    for i in range(deep):
        k = pl.program_id(0) * deep + i
        lanes = pl.ds(i * TILE, TILE)
        for half, (pattern, amp_ref) in enumerate(((mine_pattern, mine_ref), (other_pattern, other_ref))):
            for first in range(rows // second):
                value = amp_ref[pl.ds(first * second, second), lanes] * pattern[first, k].astype(jnp.float32)
                high = value.astype(jnp.bfloat16)
                low = (value - high.astype(jnp.float32)).astype(jnp.bfloat16)
                here = pl.ds(half * rows + first * second, second)
                out_ref[i, here, :TILE] = high
                out_ref[i, here, TILE:] = low


def split_amplitudes(mine, other, mine_pattern, other_pattern, lists, second, blocks):
    rows, depth = mine.shape
    tiles = depth // TILE
    deep = 4 if tiles % 4 == 0 else 1
    steps = tiles // deep
    out_shape = [jax.ShapeDtypeStruct((tiles, CORES * rows, 2 * TILE), jnp.bfloat16)]
    out_specs = [pl.BlockSpec((deep, CORES * rows, 2 * TILE), lambda k, *_: (k, 0, 0))]
    if blocks % steps == 0:
        out_shape.append(jax.ShapeDtypeStruct((rows, blocks * TILE), jnp.float32))
        out_specs.append(pl.BlockSpec((rows, blocks // steps * TILE), lambda k, *_: (0, k)))
    made = pl.pallas_call(
        functools.partial(split_kernel, second=second, deep=deep),
        grid_spec=pltpu.PrefetchScalarGridSpec(
            num_scalar_prefetch=2,
            grid=(steps,),
            in_specs=[pl.BlockSpec((rows, deep * TILE), lambda k, *_: (0, k))] * 2 + [pl.BlockSpec(memory_space=pl.ANY)],
            out_specs=out_specs,
        ),
        out_shape=out_shape,
        compiler_params=pltpu.CompilerParams(vmem_limit_bytes=VMEM_LIMIT),
        cost_estimate=pl.CostEstimate(flops=8 * rows * depth, bytes_accessed=20 * rows * depth, transcendentals=0),
    )(mine_pattern, other_pattern, mine, other, lists)
    return made if len(made) == 2 else (made[0], jnp.zeros((rows, blocks * TILE), jnp.float32))


def pack_kernel(lists_ref, *refs, plan, sources, at):
    ins, outs = refs[:sources], refs[sources:]
    for out, (base, size) in zip(outs, plan):

        def copy(slot, _, out=out, base=base):
            row = pl.multiple_of(lists_ref[at["row"] + base + slot], TILE)
            lane = pl.multiple_of(lists_ref[at["lane"] + base + slot], TILE)
            for source in range(sources):

                @pl.when(lists_ref[at["source"] + base + slot] == source)
                def _(source=source):
                    out[slot] = ins[source][pl.ds(row, TILE), pl.ds(lane, TILE)]

            return 0

        lax.fori_loop(0, size, copy, 0)


def pack(lists, at, sources, plan):
    whole = lambda x: pl.BlockSpec(x.shape, lambda g, *s: (0,) * len(x.shape))
    outs = [jax.ShapeDtypeStruct((size, TILE, TILE), jnp.float32) for _, size in plan]
    return pl.pallas_call(
        functools.partial(pack_kernel, plan=plan, sources=len(sources), at=at),
        grid_spec=pltpu.PrefetchScalarGridSpec(
            num_scalar_prefetch=1,
            grid=(1,),
            in_specs=[whole(x) for x in sources],
            out_specs=[whole(x) for x in outs],
        ),
        out_shape=outs,
        compiler_params=pltpu.CompilerParams(vmem_limit_bytes=VMEM_LIMIT),
        cost_estimate=pl.CostEstimate(
            flops=0, bytes_accessed=4 * (sum(x.size for x in sources) + sum(x.size for x in outs)), transcendentals=0
        ),
    )(lists, *sources)


def pool_kernel(lists_ref, *refs, at):
    *ins, out = refs
    for e, ref in enumerate(ins):

        def copy(slot, _, ref=ref, e=e):
            out[lists_ref[at["offsets"] + e] + slot] = ref[slot]
            return 0

        lax.fori_loop(0, lists_ref[at["sizes"] + e], copy, 0)


def pool(lists, at, arrays, capacity):
    whole = lambda shape: pl.BlockSpec(shape, lambda g, *s: (0,) * len(shape))
    shape = (capacity, TILE, TILE)
    return pl.pallas_call(
        functools.partial(pool_kernel, at=at),
        grid_spec=pltpu.PrefetchScalarGridSpec(
            num_scalar_prefetch=1,
            grid=(1,),
            in_specs=[whole(x.shape) for x in arrays],
            out_specs=whole(shape),
        ),
        out_shape=jax.ShapeDtypeStruct(shape, jnp.float32),
        compiler_params=pltpu.CompilerParams(vmem_limit_bytes=VMEM_LIMIT),
        cost_estimate=pl.CostEstimate(flops=0, bytes_accessed=12 * capacity * TILE * TILE, transcendentals=0),
    )(lists, *arrays)


def gate_kernel(*refs):
    del refs


def gate(released, awaited):
    anywhere = pl.BlockSpec(memory_space=pl.ANY)
    return pl.pallas_call(
        gate_kernel,
        in_specs=[anywhere] * (len(released) + len(awaited)),
        out_specs=[anywhere] * len(released),
        out_shape=[jax.ShapeDtypeStruct(x.shape, x.dtype) for x in released],
        input_output_aliases={i: i for i in range(len(released))},
    )(*released, *awaited)


def multiply_kernel(
    lists_ref, amp_ref, mine_in, other_in, *refs, at, turn, first, chips, segments, steps, per_chip, wide, long, straight
):
    def spot(g):
        column = g * wide
        e = column // per_chip
        return turn * chips + first + e, column - e * per_chip

    def low_of(g, i):
        listed, column = spot(g)
        return lists_ref[at["bounds"] + listed * (per_chip + 1) + column + i]

    count = len(segments)
    tiles = refs[:count]
    mine_ref, other_ref, buffer, sem = refs[count:]
    step = pl.program_id(0)
    rows = mine_ref.shape[0]

    def issue(g, half):
        low, high = low_of(g, 0), low_of(g, wide)
        for ref, (a, b, pooled, only) in zip(tiles, segments):
            shift = lists_ref[at["offsets"] + spot(g)[0]] - straight if pooled else -a

            def start(slot, _, ref=ref, shift=shift):
                pltpu.make_async_copy(
                    ref.at[slot + shift], buffer.at[half, slot - low], sem.at[half, slot - low]
                ).start()
                return 0

            first = jnp.maximum(low, a)
            last = jnp.maximum(first, jnp.minimum(high, b))
            if only is not None:
                last = jnp.where(g * wide // per_chip == only, last, first)
            lax.fori_loop(first, last, start, 0)

    half = lax.rem(step, 2)

    @pl.when(step == 0)
    def _():
        issue(0, 0)

    @pl.when(step + 1 < steps)
    def _():
        issue(step + 1, 1 - half)

    mine_ref[...] = mine_in[...]
    other_ref[...] = other_in[...]
    origin = low_of(step, 0)
    for i in range(wide):
        lanes = pl.ds(i * TILE, TILE)
        low = low_of(step, i)
        length = low_of(step, i + 1) - low
        base = at["kk"] + spot(step)[0] * long + low

        def wait(place, _, low=low):
            place = low - origin + place
            pltpu.make_async_copy(tiles[0].at[0], buffer.at[half, place], sem.at[half, place]).wait()
            return 0

        lax.fori_loop(0, length, wait, 0)

        def add(turn, _, lanes=lanes, low=low, length=length, base=base):
            weights, ks = [], []
            for u in range(UNROLL):
                place = turn * UNROLL + u
                inside = place < length
                place = jnp.minimum(place, length - 1)
                value = buffer[half, low - origin + place]
                if u:
                    value = jnp.where(inside, value, 0.0)
                high = value.astype(jnp.bfloat16)
                rest = (value - high.astype(jnp.float32)).astype(jnp.bfloat16)
                weights.append(jnp.concatenate([high, rest], axis=1))
                weights.append(jnp.concatenate([high, jnp.zeros_like(high)], axis=1))
                ks.append(lists_ref[base + place])
            left = jnp.concatenate([amp_ref[k] for k in ks], axis=1)
            product = jnp.dot(left, jnp.concatenate(weights, axis=0), preferred_element_type=jnp.float32)
            total = product[:, :TILE] + product[:, TILE:]
            mine_ref[:, lanes] += total[:rows]
            other_ref[:, lanes] += total[rows:]
            return 0

        lax.fori_loop(0, (length + UNROLL - 1) // UNROLL, add, 0)


def multiply(lists, at, turn, first, count, chips, per_chip, wide, long, straight, amps, mine, other, pieces, kd, spot):
    rows = mine.shape[0]
    segments = [piece[1:] for piece in pieces]
    blocks = per_chip // wide
    steps = count * blocks
    expected = 10 * steps * wide
    n = 1
    mine_spec = pl.BlockSpec((rows, wide * TILE), lambda g, s: (0, s[at["mine"] + first * blocks + g]))
    other_spec = pl.BlockSpec((rows, wide * TILE), lambda g, s: (0, spot * blocks + g))
    anywhere = pl.BlockSpec(memory_space=pl.ANY)
    held = CORES * kd * wide
    return pl.pallas_call(
        functools.partial(
            multiply_kernel,
            at=at,
            turn=turn,
            first=first,
            chips=chips,
            segments=segments,
            steps=steps,
            per_chip=per_chip,
            wide=wide,
            long=long,
            straight=straight,
        ),
        grid_spec=pltpu.PrefetchScalarGridSpec(
            num_scalar_prefetch=n,
            grid=(steps,),
            in_specs=[
                pl.BlockSpec((CORES * kd, CORES * rows, 2 * TILE), lambda g, s: (s[at["planes"] + turn], 0, 0)),
                mine_spec,
                other_spec,
            ]
            + [anywhere] * len(pieces),
            out_specs=[mine_spec, other_spec],
            scratch_shapes=[pltpu.VMEM((2, held, TILE, TILE), jnp.float32), pltpu.SemaphoreType.DMA((2, held))],
        ),
        out_shape=[jax.ShapeDtypeStruct(x.shape, x.dtype) for x in (mine, other)],
        input_output_aliases={n + 1: 0, n + 2: 1},
        compiler_params=pltpu.CompilerParams(vmem_limit_bytes=VMEM_LIMIT),
        cost_estimate=pl.CostEstimate(
            flops=expected * 32 * rows * TILE * TILE,
            bytes_accessed=expected * 4 * TILE * TILE,
            transcendentals=0,
        ),
    )(lists, amps, mine, other, *[piece[0] for piece in pieces])


def place_kernel(at_ref, mine_in, piece_ref, out_ref):
    out_ref[...] = mine_in[...] + piece_ref[...]


def place(at, wide, mine, piece):
    rows = mine.shape[0]
    spec = pl.BlockSpec((rows, wide * TILE), lambda g, a: (0, a[g]))
    return pl.pallas_call(
        place_kernel,
        grid_spec=pltpu.PrefetchScalarGridSpec(
            num_scalar_prefetch=1,
            grid=(at.shape[0],),
            in_specs=[spec, pl.BlockSpec((rows, wide * TILE), lambda g, a: (0, g))],
            out_specs=spec,
        ),
        out_shape=jax.ShapeDtypeStruct(mine.shape, mine.dtype),
        input_output_aliases={1: 0},
        compiler_params=pltpu.CompilerParams(vmem_limit_bytes=VMEM_LIMIT),
        cost_estimate=pl.CostEstimate(flops=piece.size, bytes_accessed=12 * piece.size, transcendentals=0),
    )(at, mine, piece)


def body(amplitudes, integrals, amp_pattern, int_pattern, *, chips, devices):
    R, Z = chips, devices // CORES
    first, second, depth = amplitudes.shape
    rows = first * second
    kd = integrals.shape[0] // TILE
    ntl = integrals.shape[1] // TILE
    groups = R if ntl % R == 0 else 1
    width = ntl // groups
    if groups == 4:
        wide = width
        owned = [[d * width + i for d in pair for i in range(width)] for pair in ((0, 3), (1, 2))]
    else:
        wide = 1
        owned = [list(range(c, ntl, CORES)) for c in range(CORES)]
        owned = [x + [ntl] * (len(owned[0]) - len(x)) for x in owned]
    per_chip = len(owned[0])
    tiles = per_chip * CORES * kd

    r = lax.axis_index("row")
    col = lax.axis_index("col")
    core = lax.rem(col, CORES)
    ring = [0] + list(range(1, Z, 2)) + [z for z in range(Z - 1, 0, -1) if z % 2 == 0]
    spot = [ring.index(z) for z in range(Z)]

    def by_row(x, distance):
        return lax.ppermute(x, "row", [(a, a ^ distance) for a in range(R)])

    def by_core(x):
        return lax.ppermute(x, "col", [(a, a ^ 1) for a in range(Z * CORES)])

    def by_plane(x):
        return lax.ppermute(
            x,
            "col",
            [(ring[a] * CORES + c, ring[(a + 1) % Z] * CORES + c) for a in range(Z) for c in range(CORES)],
        )

    blocks = R * ntl
    spare = per_chip * CORES - ntl
    parts_of = [[0], [1, 2], [3]] if R == 4 else [list(range(R))]
    others = [jnp.zeros((rows, len(part) * per_chip * TILE), jnp.float32) for part in parts_of]
    shares = [integrals[:, d * width * TILE : (d + 1) * width * TILE] for d in range(groups)]
    if groups > 1:
        (int_pattern,) = gate([int_pattern], shares[1:])
    for d in range(1, groups):
        shares[d] = by_row(shares[d], d)

    patterns = [int_pattern] + [by_row(int_pattern, d) for d in range(1, R)]
    by_distance = jnp.stack(patterns).reshape(R, Z, CORES * kd, groups, width)
    near = []
    for e in range(R):
        picked = jnp.stack([by_distance[e ^ d, :, :, d] for d in range(groups)], axis=2)
        near.append(picked.reshape(Z, CORES * kd, ntl))
    present = (jnp.stack(near, axis=1) != 0).astype(jnp.int32)
    present = jnp.pad(present, ((0, 0), (0, 0), (0, 0), (0, per_chip * CORES - ntl)))
    present = jnp.stack([jnp.stack([present[..., j] for j in x], axis=-1) for x in owned], axis=-1)
    present = present.transpose(0, 1, 4, 3, 2)
    both = present.reshape(Z, R, CORES, tiles)
    cores_counts = jnp.sum(both, axis=-1)
    own = jnp.where(core == 0, both[:, :, 0], both[:, :, 1])
    here = jnp.asarray(spot)[col // CORES]
    planes = jnp.asarray(ring)[lax.rem(here - jnp.arange(Z) + Z, Z)]
    if R == 4:
        own = jnp.stack(
            [
                own[:, 0],
                jnp.where(core == 0, own[:, 1], own[:, 2]),
                jnp.where(core == 0, own[:, 2], own[:, 1]),
                own[:, 3],
            ],
            axis=1,
        )
    own = own[planes]
    counts = jnp.sum(own, axis=-1)
    ids = jnp.arange(tiles)
    slot_of = jnp.sum(own[..., None, :] * (ids[None, :] < ids[:, None]), axis=-1)
    slots = (
        jnp.sum(
            (ids + 1)[None, None, None, :]
            * ((slot_of[:, :, None, :] == ids[:, None]) & (own[:, :, None, :] > 0)),
            axis=-1,
        )
        - 1
    )
    ends = jnp.sum(own[:, :, None, :] * (ids[None, :] < (jnp.arange(per_chip + 1) * CORES * kd)[:, None]), axis=-1)

    straight = max(2, round(tiles * 38 / 72)) if R == 4 else max(4, 2 * round(tiles * 25 / 72))
    extra = max(2, round(tiles * 12 / 72)) if R == 4 else 0
    pooled = max(R, round(tiles * 20 / 72)) if R == 4 else 0
    longest = tiles + straight + extra
    slots = jnp.pad(slots, ((0, 0), (0, 0), (0, longest - tiles)), constant_values=-1)
    most = jnp.max(cores_counts)

    def chips_of(which):
        return r ^ (jnp.stack([0 * which, 1 + which, 2 - which, 0 * which + 3]) if R == 4 else jnp.arange(R))

    chip_of = chips_of(core)

    def columns_of(which):
        column = jnp.asarray(owned)[which][None, ::wide]
        group = column // width
        chip = chips_of(which)[:, None]
        at = (((chip ^ group) if groups > 1 else chip) * groups + group) * width + column % width
        return (jnp.where(column < ntl, at, blocks) // wide).astype(jnp.int32)

    mine_at = columns_of(core)
    received_at = columns_of(1 - core)

    def across(x, near):
        return lax.ppermute(
            x,
            ("row", "col"),
            [
                (a * devices + d, (a ^ (near if d % CORES == 0 else 3 - near)) * devices + d)
                for a in range(R)
                for d in range(devices)
            ],
        )

    def listed(base):
        after = base + straight
        left = jnp.clip(cores_counts - after, 0, extra)
        fits = jnp.max(jnp.sum(left, axis=1)) <= pooled
        taken = jnp.where(fits, extra, pooled // R) if extra else jnp.int32(0)
        sizes = jnp.clip(counts - after, 0, taken)
        before = chip_of[None, :] < chip_of[:, None]
        offsets = jnp.sum(sizes[:, None, :] * before[None], axis=-1)
        now = lax.dynamic_slice_in_dim(slots, base, straight + extra, axis=2)
        kk = jnp.maximum(now, 0) % (CORES * kd)
        bounds = jnp.clip(ends - base, 0, straight + taken)
        column = jnp.asarray(owned)[core][jnp.maximum(now[0, 0], 0) // (CORES * kd)]
        holder = kk[0, 0] // kd
        source = jnp.where(now[0, 0] < 0, -1, (holder != core) * groups + column // width)
        found = {
            "source": source,
            "row": kk[0, 0] % kd * TILE,
            "lane": column % width * TILE,
            "sizes": sizes,
            "offsets": offsets,
            "bounds": bounds,
            "kk": kk,
            "mine": mine_at,
            "planes": planes,
        }
        at, total = {}, 0
        for name, x in found.items():
            at[name] = total
            total += x.size
        return jnp.concatenate([x.reshape(-1).astype(jnp.int32) for x in found.values()]), at, taken

    first_lists = listed(jnp.int32(0))
    amps_mine = amplitudes.reshape(rows, depth)
    amps, mine = split_amplitudes(
        amps_mine, by_core(amps_mine), amp_pattern, by_core(amp_pattern), first_lists[0], second, blocks + spare
    )
    if groups > 1:
        shares[1:] = gate(shares[1:], [amps])
    twins = [by_core(x) for x in shares]

    def one_round(state, others, made):
        base, mine = state
        others = list(others)
        lists, at, taken = made
        plan = ((0, straight), (straight, extra), (0, straight)) if extra else ((0, straight),)
        packed = pack(lists, at, shares + twins, plan)

        def add(mine, other, step, neighbours, pieces, spot=0):
            return multiply(
                lists,
                at,
                step,
                neighbours[0],
                len(neighbours),
                R,
                per_chip,
                wide,
                straight + extra,
                straight,
                amps,
                mine,
                other,
                pieces,
                kd,
                spot,
            )

        if R == 4:
            end = straight + extra
            sent, late, ready = packed
            along = [sent, by_plane(sent)]
            first_late, second_late = across(late, 1), across(late, 2)
            at_home = [(sent, 0, straight, False, None), (late, straight, end, False, None)]
            mine, others[0] = add(mine, others[0], 0, [0], at_home)
            first_late, ready, mine = gate([first_late, ready, mine], [second_late])
            third_late = across(first_late, 2)
            first_near, second_near = across(ready, 1), across(ready, 2)
            pools = [
                pool(
                    lists,
                    at,
                    [late, first_late, second_late, third_late],
                    pooled,
                )
            ]
            pools.append(by_plane(pools[0]))
            received = []
            for step in range(Z):
                mixed = (pools[step], straight, end, True, None)
                if step:
                    home = [(along[step], 0, straight, False, None), mixed]
                    mine, others[0] = add(mine, others[0], step, [0], home)
                if step == Z - 1:
                    received.append(by_core(others[0]))
                first_near, mine = gate([first_near, mine], [second_near, pools[step], along[step if step else 1]])
                third_near = across(first_near, 2)
                near = [(first_near, 0, straight, False, 0), (second_near, 0, straight, False, 1), mixed]
                last = [(third_near, 0, straight, False, None), mixed]
                mine, others[1] = add(mine, others[1], step, [1, 2], near)
                if step == Z - 1:
                    received.append(by_core(others[1]))
                    mine = place(received_at[0], wide, mine, received[0])
                else:
                    along[step + 1], pools[step + 1], mine = gate(
                        [along[step + 1], pools[step + 1], mine], [third_near]
                    )
                    first_near, second_near = across(along[step + 1], 1), across(along[step + 1], 2)
                    if step + 2 < Z:
                        along.append(by_plane(along[step + 1]))
                        pools.append(by_plane(pools[step + 1]))
                mine, others[2] = add(mine, others[2], step, [3], last)
            received.append(by_core(others[2]))
            mine = place(received_at[1:3].reshape(-1), wide, mine, received[1])
            mine = place(received_at[3], wide, mine, received[2])
        else:
            now_at = packed[0]
            for step in range(Z):
                for e in range(R):
                    piece = by_row(now_at, e) if e else now_at
                    mine, others[0] = add(mine, others[0], step, [e], [(piece, 0, straight, False, None)], e)
                if step + 1 < Z:
                    now_at = by_plane(now_at)
            mine = place(received_at.reshape(-1), wide, mine, by_core(others[0]))
        return base + straight + taken, mine

    state = one_round((jnp.int32(0), mine), others, first_lists)
    cleared = [x.shape for x in others]
    _, mine = lax.while_loop(
        lambda state: state[0] < most,
        lambda state: one_round(state, [jnp.zeros(shape, jnp.float32) for shape in cleared], listed(state[0])),
        state,
    )
    return mine[:, : blocks * TILE].reshape(first, second, blocks * TILE)


def solution(mesh):
    placed = (P("col", "row", None), P("col", "row"), P("col", None), P(None, "row"))
    return jax.shard_map(
        functools.partial(body, chips=mesh.shape["row"], devices=mesh.shape["col"]),
        mesh=mesh,
        in_specs=placed,
        out_specs=P("col", "row", None),
        check_vma=False,
    )
```
